32 devices in a mesh: dp: 4 (over y, x), expert: 4 (over z), tensor: 2 (over core).
Axes of the slice: x: 2, y: 2, z: 4, core: 2. Of those that a mesh axis runs over, the one named last changes fastest.
Arguments:
- tokens: bfloat16 [2048, 2048], P(('dp', 'expert')), may hold values from -6 to 6
- expert_ids: int32 [2048, 2], P(('dp', 'expert')), may hold values from 0 to 3, all different within a row; in each aligned block of 128 rows (0 to 127, 128 to 255, ...) at most 96 rows name the same one
- gate_values: float32 [2048, 2], P(('dp', 'expert')), may hold values from 0.1 to 1
- tag_labels: int32 [2048], P(('dp', 'expert')), may hold values from 0 to 31
- w_gate: bfloat16 [4, 2048, 7168], P('expert', 'dp', 'tensor'), may hold values from -0.125 to 0.125
- w_up: bfloat16 [4, 2048, 7168], P('expert', 'dp', 'tensor'), may hold values from -0.125 to 0.125
- w_down: bfloat16 [4, 7168, 2048], P('expert', 'tensor', 'dp'), may hold values from -0.0625 to 0.0625
- adapter_in: bfloat16 [4, 16, 2048], P('expert'), may hold values from -0.125 to 0.125
- adapter_out: bfloat16 [4, 16, 7168], P('expert', None, 'tensor'), may hold values from -1.5 to 1.5
- tag_weight: bfloat16 [2048, 32], replicated, may hold values from -0.125 to 0.125
Outputs:
- layer_out: bfloat16 [2048, 2048], P(('dp', 'expert'), 'tensor')
- in_gradient: float32 [4, 16, 2048], P('expert')
- out_gradient: float32 [4, 16, 7168], P('expert', None, 'tensor')
The draws below stay inside these ranges and needn't reach their ends.
Inputs may be any that keep to these rules, and one draw needn't show every extreme that they name: `expert_ids`: each row names 2 different experts; the rows of one index of dp and expert name each expert at most 96 times, a bound that some block reaches.
All inputs are finite; a program needn't handle non-finite values.
Results may differ from the reference program's by a relative error of at most 0.017.
Values may be sent and summed in bfloat16 or wider, within the bound.
No kernel may reach another device: no remote copies, remote signals or barrier semaphores. Data moves between devices by JAX's collectives and lax.ppermute only.
A program may use at most 128 MiB of HBM per device.

```python
import math
import jax
import jax.numpy as jnp
import numpy as np
from jax import lax

D = 2048
FF = 7168
RANK = 16
TOP = 2
TAGS = 32
TOK_DEV = 128
EXPERTS = 4
CAP = 96
TOKENS = 2048


def with_ends(values, rng, low, largest):
    longest = values.shape.index(max(values.shape))
    spots = []
    for shift in (0, 1):
        where = [jax.random.randint(jax.random.fold_in(rng, axis), (), 0, length) for axis, length in enumerate(values.shape)]
        where[longest] = (where[longest] + shift) % values.shape[longest]
        spots.append(tuple(where))
    return values.at[spots[0]].set(low).at[spots[1]].set(largest)


def block_scale(key, extent, cuts, smallest, high):
    level = 1.0
    for axis_at, blocks in cuts:
        draws = jax.random.uniform(jax.random.fold_in(jax.random.fold_in(key, 6), axis_at), (blocks,), jnp.float32, smallest / len(cuts), high / len(cuts))
        level = level * jnp.repeat(jnp.exp(draws), extent[axis_at] // blocks).reshape((-1,) + (1,) * (len(extent) - 1 - axis_at))
    return level


def assign_block(rng, own, number, rows, count, top, limit, lean):
    sequence = jax.random.permutation(rng, count)
    heavy_load, ordinary = portions_of(count, rows * top, limit, lean, True), portions_of(count, rows * top, limit, lean, False)
    places = jnp.arange(count)

    def named(sizes, offset_by):
        used = int((sizes > 0).sum())
        fixed = max(1, used // 4)
        passed = fixed + (places - fixed + offset_by * (used - fixed)) % max(1, count - fixed)
        return jnp.zeros((count,), jnp.int32).at[sequence[jnp.where(places < fixed, places, passed)]].set(jnp.asarray(sizes, jnp.int32))

    sizes = jnp.where(number % 4 == 0, named(heavy_load, number // 4), named(ordinary, number - number // 4 - 1))
    mixed = jax.random.permutation(jax.random.fold_in(own, 3), count)
    giver, taker = mixed[0:count // 2 * 2:2], mixed[1:count // 2 * 2:2]
    margin = jnp.minimum(sizes[giver] - 1, limit - sizes[taker]) // 2
    margin = jnp.where((giver == sequence[0]) | (taker == sequence[0]) | (sizes[taker] == 0), 0, jnp.maximum(margin, 0))
    passed = jax.random.randint(jax.random.fold_in(own, 4), (count // 2,), 0, 1 << 20) % (margin + 1)
    sizes = sizes.at[giver].add(-passed).at[taker].add(passed)
    items = jnp.searchsorted(jnp.cumsum(sizes), jnp.arange(rows * top), side="right").astype(jnp.int32)
    grid = items.reshape(top, rows).T
    grid = grid[jax.random.permutation(jax.random.fold_in(own, 1), rows)]
    offset_by = jax.random.randint(jax.random.fold_in(own, 2), (rows, 1), 0, top)
    return jnp.take_along_axis(grid, (jnp.arange(top)[None, :] + offset_by) % top, axis=1)


def portions_of(count, total, limit, slope, full):
    loads = [(1 << 20) // math.isqrt(grade ** slope) + 1 for grade in range(1, count + 1)]
    largest = limit if full else min(limit, max(-(-total // count), total * loads[0] // sum(loads)))
    least = 1 if total - largest >= count - 1 else 0
    counts, rest = [largest] + [least] * (count - 1), total - largest - least * (count - 1)
    while rest > 0:
        free = [i for i in range(1, count) if counts[i] < largest] or [i for i in range(1, count) if counts[i] < limit]
        pool, remaining = sum([loads[i] for i in free]), rest
        for i in free:
            addition = min(limit - counts[i], max(1, remaining * loads[i] // pool), rest)
            counts[i] = counts[i] + addition
            rest = rest - addition
    return np.array(counts)


def centred(stream_key, shape, spread, reach, cuts=(), kind=jnp.bfloat16):
    level = block_scale(stream_key, shape, cuts, -0.22, 0.18) if cuts else 1.0
    entries = jax.random.normal(stream_key, shape, jnp.float32) * spread * level
    return jnp.minimum(jnp.maximum(entries, -reach), reach).astype(kind)


def setup_inputs(seed: int = 0) -> dict:
    key_list = jax.random.split(jax.random.key(seed), 11)
    tokens = centred(key_list[0], (TOKENS, D), 1.0, 6.0, ((0, 16),))
    expert_ids_keys = jax.random.split(jax.random.fold_in(key_list[1], 1), TOKENS // TOK_DEV)
    expert_ids_turns = jax.random.permutation(jax.random.fold_in(key_list[1], 3), TOKENS // TOK_DEV)
    expert_ids = jax.vmap(lambda own, number: assign_block(jax.random.fold_in(key_list[1], 2), own, number, TOK_DEV, EXPERTS, TOP, CAP, 2))(expert_ids_keys, expert_ids_turns).reshape((TOKENS, TOP))
    gate_values = jnp.clip(0.1 + 0.9 * jax.random.uniform(key_list[2], (TOKENS, TOP), jnp.float32) ** block_scale(key_list[2], (TOKENS, TOP), ((0, 16),), -0.2, 0.2), 0.1, 1.0)
    tag_labels = with_ends(jax.random.randint(key_list[3], (TOKENS,), 0, TAGS), jax.random.fold_in(key_list[3], 1), 0, TAGS - 1).astype(jnp.int32)
    w_gate = centred(key_list[4], (EXPERTS, D, FF), D ** -0.5, 0.125, ((0, 4), (1, 4), (2, 2)))
    w_up = centred(key_list[5], (EXPERTS, D, FF), D ** -0.5, 0.125, ((0, 4), (1, 4), (2, 2)))
    w_down = centred(key_list[6], (EXPERTS, FF, D), FF ** -0.5, 0.0625, ((0, 4), (1, 2), (2, 4)))
    adapter_in = centred(key_list[7], (EXPERTS, RANK, D), D ** -0.5, 0.125, ((0, 4),))
    adapter_out = centred(key_list[8], (EXPERTS, RANK, FF), RANK ** -0.5, 1.5, ((0, 4), (2, 2)))
    tag_weight = centred(key_list[9], (D, TAGS), D ** -0.5, 0.125)
    return {"tokens": tokens, "expert_ids": expert_ids, "gate_values": gate_values, "tag_labels": tag_labels, "w_gate": w_gate, "w_up": w_up, "w_down": w_down, "adapter_in": adapter_in, "adapter_out": adapter_out, "tag_weight": tag_weight}


adapter_scale = 2.0


def reference(tokens, expert_ids, gate_values, tag_labels, w_gate, w_up, w_down, adapter_in, adapter_out, tag_weight):
    rows_limit = (TOKENS // TOK_DEV) * CAP
    combined = tokens.astype(jnp.float32)
    stored = []
    for expert in range(EXPERTS):
        chosen = expert_ids == expert
        weight_token = jnp.sum(jnp.where(chosen, gate_values, jnp.float32(0.0)), axis=1)
        member = jnp.any(chosen, axis=1)
        picked = jnp.nonzero(member, size=rows_limit, fill_value=0)[0].astype(jnp.int32)
        valid_row = jnp.arange(rows_limit, dtype=jnp.int32) < jnp.sum(member.astype(jnp.int32))
        row_values = jnp.where(valid_row[:, None], tokens[picked], jnp.zeros((), jnp.bfloat16))
        row_weights = jnp.where(valid_row, weight_token[picked], jnp.float32(0.0))
        gate_acc = jnp.dot(row_values, w_gate[expert], preferred_element_type=jnp.float32)
        low_rank = jnp.dot(row_values, adapter_in[expert].T, preferred_element_type=jnp.float32).astype(jnp.bfloat16)
        up_full = jnp.dot(row_values, w_up[expert], preferred_element_type=jnp.float32) + adapter_scale * jnp.dot(low_rank, adapter_out[expert], preferred_element_type=jnp.float32)
        activated = jax.nn.silu(gate_acc)
        hidden = (activated * up_full).astype(jnp.bfloat16)
        result = jnp.dot(hidden, w_down[expert], preferred_element_type=jnp.float32).astype(jnp.bfloat16)
        combined = combined.at[picked].add(row_weights[:, None] * result.astype(jnp.float32))
        stored.append((picked, row_weights, row_values, low_rank, activated))
    layer_out = combined.astype(jnp.bfloat16)
    logits = jnp.dot(layer_out, tag_weight, preferred_element_type=jnp.float32)
    exp_logits = jnp.exp(logits)
    probability = exp_logits / jnp.sum(exp_logits, axis=1, keepdims=True)
    labels_hot = (tag_labels[:, None] == jnp.arange(TAGS, dtype=jnp.int32)[None, :]).astype(jnp.float32)
    logit_grad = probability - labels_hot
    upstream = jnp.dot(logit_grad, tag_weight.astype(jnp.float32).T, precision=lax.Precision.HIGHEST)
    in_list = []
    out_list = []
    for expert in range(EXPERTS):
        picked, row_weights, row_values, low_rank, activated = stored[expert]
        slot_grad = (row_weights[:, None] * upstream[picked]).astype(jnp.bfloat16)
        hidden_grad = jnp.dot(slot_grad, w_down[expert].T, preferred_element_type=jnp.float32)
        up_grad = (hidden_grad * activated).astype(jnp.bfloat16)
        out_list.append(adapter_scale * jnp.dot(low_rank.T, up_grad, preferred_element_type=jnp.float32))
        low_grad = adapter_scale * jnp.dot(up_grad, adapter_out[expert].T, preferred_element_type=jnp.float32)
        in_list.append(jnp.dot(low_grad.T, row_values.astype(jnp.float32), precision=lax.Precision.HIGHEST))
    return layer_out, jnp.stack(in_list), jnp.stack(out_list)
```

```python
import jax
import jax.numpy as jnp
from jax import lax
from jax.sharding import PartitionSpec as P

adapter_scale = 2.0
f32 = jnp.float32
bf16 = jnp.bfloat16
highest = lax.Precision.HIGHEST


def partner(index, step, count):
    if count & (count - 1) == 0:
        return index ^ step, index ^ step
    return (index + step) % count, (index - step) % count


def send(value, axis, step):
    count = lax.axis_size(axis)
    return lax.ppermute(value, axis, [(i, partner(i, step, count)[0]) for i in range(count)])


def exchange(pieces, axis):
    count, me = lax.axis_size(axis), lax.axis_index(axis)
    own = lax.dynamic_slice_in_dim(pieces, me, 1, 0)
    result = lax.dynamic_update_slice_in_dim(jnp.zeros_like(pieces), own, me, 0)
    for step in range(1, count):
        target, source = partner(me, step, count)
        came = send(lax.dynamic_slice_in_dim(pieces, target, 1, 0), axis, step)
        result = lax.dynamic_update_slice_in_dim(result, came, source, 0)
    return result


def exchange_sum(pieces, axis):
    count, me = lax.axis_size(axis), lax.axis_index(axis)
    total = lax.dynamic_index_in_dim(pieces, me, 0, keepdims=False).astype(f32)
    for step in range(1, count):
        target, _ = partner(me, step, count)
        total = total + send(lax.dynamic_index_in_dim(pieces, target, 0, keepdims=False), axis, step).astype(f32)
    return total


def gather(value, axis):
    count, me = lax.axis_size(axis), lax.axis_index(axis)
    result = jnp.zeros((count,) + value.shape, value.dtype)
    result = lax.dynamic_update_slice_in_dim(result, value[None], me, 0)
    for step in range(1, count):
        _, source = partner(me, step, count)
        result = lax.dynamic_update_slice_in_dim(result, send(value, axis, step)[None], source, 0)
    return result


def gather_sum(value, axis):
    total = value.astype(f32)
    for step in range(1, lax.axis_size(axis)):
        total = total + send(value, axis, step).astype(f32)
    return total


def dot(left, right, left_dim, right_dim, **options):
    return lax.dot_general(
        left, right, (((left_dim,), (right_dim,)), ((), ())), preferred_element_type=f32, **options
    )


def local(
    tokens,
    expert_ids,
    gate_values,
    tag_labels,
    w_gate,
    w_up,
    w_down,
    adapter_in,
    adapter_out,
    tag_weight,
):
    experts = lax.axis_size("expert")
    shards = lax.axis_size("tensor")
    groups = lax.axis_size("dp")
    dp, tensor = lax.axis_index("dp"), lax.axis_index("tensor")
    tok_count, model_width = tokens.shape
    share_width = model_width // shards
    capacity = 3 * tok_count // experts
    feature_part = w_gate.shape[1]
    hidden_part = w_gate.shape[2] // groups
    tags = tag_weight.shape[1]
    rank = adapter_in.shape[1]
    slots = experts * groups * capacity

    member = expert_ids[None, :, :] == jnp.arange(experts, dtype=jnp.int32)[:, None, None]
    used = jnp.any(member, axis=2).astype(f32)
    weight = jnp.sum(jnp.where(member, gate_values[None], f32(0.0)), axis=2)
    upto = (jnp.arange(tok_count)[:, None] <= jnp.arange(tok_count)[None, :]).astype(f32)
    code = used * dot(used, upto, 1, 0)
    places = jnp.arange(1, capacity + 1, dtype=f32)
    own_match = code[:, None, :] == places[None, :, None]
    combine = jnp.where(own_match, weight[:, None, :], f32(0.0)).reshape(experts * capacity, tok_count)

    token_half = lax.dynamic_slice_in_dim(tokens, tensor * share_width, share_width, 1)
    code_rows = jnp.pad(code.astype(bf16), ((0, 16 - experts), (0, share_width - tok_count)))
    plane = gather(jnp.concatenate([token_half, code_rows], axis=0), "dp")
    plane_code = plane[:, tok_count : tok_count + experts, :tok_count].astype(f32)
    match = (plane_code[:, :, None, :] == places[None, None, :, None]).astype(bf16)
    outgoing = jnp.einsum(
        "gest,gtd->egsd", match, plane[:, :tok_count], preferred_element_type=f32
    ).astype(bf16)
    x_half = exchange(outgoing, "expert").reshape(slots, share_width)
    x_other = send(x_half, "tensor", 1)
    x = jnp.zeros((slots, model_width), bf16)
    x = lax.dynamic_update_slice_in_dim(x, x_half, tensor * share_width, 1)
    x = lax.dynamic_update_slice_in_dim(x, x_other, (1 - tensor) * share_width, 1)

    tag_part = lax.dynamic_slice_in_dim(tag_weight, dp * feature_part, feature_part, 0)
    tag_down = dot(tag_part, w_down[0], 0, 1).astype(bf16)
    tag_down = exchange_sum(tag_down.reshape(tags, groups, hidden_part).transpose(1, 0, 2), "dp").astype(bf16)

    gate_up = jnp.stack(
        [w_gate[0].reshape(feature_part, groups, hidden_part), w_up[0].reshape(feature_part, groups, hidden_part)], axis=2
    )
    gate_up = gate_up.reshape(feature_part, groups, 2 * hidden_part).transpose(1, 0, 2)
    gate_up = exchange(gate_up, "dp").reshape(model_width, 2 * hidden_part)
    down = exchange(w_down[0].reshape(groups, hidden_part, feature_part), "dp")
    adapter_part = lax.dynamic_slice_in_dim(adapter_out[0], dp * hidden_part, hidden_part, 1)

    product = dot(x, gate_up, 1, 0)
    low_rank = dot(x, adapter_in[0], 1, 1).astype(bf16)
    activated = jax.nn.silu(product[:, :hidden_part])
    hidden = (
        activated * (product[:, hidden_part:] + adapter_scale * dot(low_rank, adapter_part, 1, 0))
    ).astype(bf16)
    activated = activated.astype(bf16)

    slot_logits = dot(tag_down, hidden, 1, 1)
    slot_logits = slot_logits + send(slot_logits.astype(bf16), "tensor", 1).astype(f32)
    slot_logits = slot_logits.reshape(tags, experts, groups, capacity).transpose(2, 1, 0, 3).astype(bf16)
    slot_logits = exchange_sum(slot_logits, "dp").astype(bf16)
    slot_logits = exchange(slot_logits, "expert").transpose(1, 0, 2).reshape(tags, experts * capacity)
    logits = dot(tag_weight, tokens, 0, 1) + dot(slot_logits.astype(f32), combine, 1, 0, precision=highest)
    exp_logits = jnp.exp(logits)
    probability = exp_logits / jnp.sum(exp_logits, axis=0, keepdims=True)
    labels_hot = (tag_labels[None, :] == jnp.arange(tags, dtype=jnp.int32)[:, None]).astype(f32)
    logit_grad = probability - labels_hot
    slot_grad = dot(logit_grad, combine, 1, 1, precision=highest).astype(bf16)
    slot_grad = exchange(slot_grad.reshape(tags, experts, capacity).transpose(1, 0, 2), "expert")
    slot_grad = gather(slot_grad, "dp").transpose(2, 1, 0, 3).reshape(tags, slots)

    up_grad = (dot(slot_grad, tag_down, 0, 0) * activated.astype(f32)).astype(bf16)
    out_local = adapter_scale * dot(low_rank, up_grad, 0, 0)
    low_grad = (adapter_scale * dot(up_grad, adapter_part, 1, 1)).astype(bf16)
    in_local = dot(low_grad, x, 0, 0)
    in_local = in_local + send(in_local.astype(bf16), "tensor", 1).astype(f32)
    in_total = gather_sum(in_local.astype(bf16), "dp")
    out_total = gather(out_local, "dp").transpose(1, 0, 2).reshape(rank, groups * hidden_part)

    half = groups // shards
    down_own = lax.dynamic_slice_in_dim(down, tensor * half, half, 0)
    down_other = lax.dynamic_slice_in_dim(down, (1 - tensor) * half, half, 0)
    other = dot(hidden, down_other, 1, 1).astype(bf16)
    own = dot(hidden, down_own, 1, 1) + send(other, "tensor", 1).astype(f32)
    own = own.reshape(experts, groups, capacity, share_width).transpose(1, 0, 2, 3).astype(bf16)
    returned = exchange_sum(own, "dp").astype(bf16)
    returned = exchange(returned, "expert").reshape(experts * capacity, share_width)
    layer_out = token_half.astype(f32) + dot(combine, returned.astype(f32), 0, 0, precision=highest)
    return (layer_out.astype(bf16), in_total[None], out_total[None])


def solution(mesh):
    in_specs = (
        P(("dp", "expert"), None),
        P(("dp", "expert"), None),
        P(("dp", "expert"), None),
        P(("dp", "expert")),
        P("expert", "dp", "tensor"),
        P("expert", "dp", "tensor"),
        P("expert", "tensor", "dp"),
        P("expert", None, None),
        P("expert", None, "tensor"),
        P(),
    )
    out_specs = (
        P(("dp", "expert"), "tensor"),
        P("expert", None, None),
        P("expert", None, "tensor"),
    )
    return jax.shard_map(local, mesh=mesh, in_specs=in_specs, out_specs=out_specs, check_vma=False)
```

```python
import functools

import jax
import jax.numpy as jnp
from jax import lax
from jax.experimental import pallas as pl
from jax.experimental.pallas import tpu as pltpu
from jax.sharding import PartitionSpec as P

adapter_scale = 2.0
f32 = jnp.float32
bf16 = jnp.bfloat16
highest = lax.Precision.HIGHEST
vmem_limit = 50 * 1024 * 1024


def partner(index, step, count):
    if count & (count - 1) == 0:
        return index ^ step, index ^ step
    return (index + step) % count, (index - step) % count


def send(value, axis, step):
    count = lax.axis_size(axis)
    return lax.ppermute(value, axis, [(i, partner(i, step, count)[0]) for i in range(count)])


def gather(value, axis):
    return [value] + [send(value, axis, step) for step in range(1, lax.axis_size(axis))]


def total(values):
    result = values[0].astype(f32)
    for value in values[1:]:
        result = result + value.astype(f32)
    return result


def dot(left, right, left_dim, right_dim, **options):
    return lax.dot_general(
        left, right, (((left_dim,), (right_dim,)), ((), ())), preferred_element_type=f32, **options
    )


def row_copies(place, own, other, scratch, sems, step, per_block, start):
    rows, width = scratch.shape[1], own[0].shape[1]
    slot = lax.rem(step, 2)
    first = pl.multiple_of(lax.rem(step, per_block) * rows, rows)

    def both(block):
        for half, (ref, side) in enumerate(((own[block], place[1]), (other[block], 1 - place[1]))):
            column = pl.multiple_of(side * width, width)
            copy = pltpu.make_async_copy(
                ref.at[pl.ds(first, rows)],
                scratch.at[slot, :, pl.ds(column, width)],
                sems.at[slot, half],
            )
            copy.start() if start else copy.wait()

    if start:
        for block in range(len(own)):
            pl.when(step // per_block == block)(functools.partial(both, block))
    else:
        both(0)


def forward_kernel(
    groups, experts, per_block, place, *refs
):
    refs = list(refs)
    own = [refs.pop(0) for _ in range(experts)]
    other = [refs.pop(0) for _ in range(experts)]
    gates = [refs.pop(0) for _ in range(groups)]
    ups = [refs.pop(0) for _ in range(groups)]
    adapter_in, adapter_part, tag_down = refs[:3]
    hidden, activated, low_rank, slot_logits = refs[3:7]
    gate, up, x_scratch, weight_sems, x_sems = refs[7:]
    step, steps = pl.program_id(0), pl.num_programs(0)
    depth = gates[0].shape[0]

    def weight_copies():
        for k in range(groups):
            _, source = partner(place[0], k, groups)
            row = pl.ds(pl.multiple_of(source * depth, depth), depth)
            yield pltpu.make_async_copy(gates[k], gate.at[row], weight_sems.at[0, k])
            yield pltpu.make_async_copy(ups[k], up.at[row], weight_sems.at[1, k])

    @pl.when(step == 0)
    def _():
        row_copies(place, own, other, x_scratch, x_sems, step, per_block, True)
        for copy in weight_copies():
            copy.start()

    @pl.when(step + 1 < steps)
    def _():
        row_copies(place, own, other, x_scratch, x_sems, step + 1, per_block, True)

    row_copies(place, own, other, x_scratch, x_sems, step, per_block, False)

    @pl.when(step == 0)
    def _():
        for copy in weight_copies():
            copy.wait()

    x = x_scratch[lax.rem(step, 2)]
    low = dot(x, adapter_in[...], 1, 1).astype(bf16)
    low_rank[...] = low
    gate_acc = dot(x, gate[...], 1, 0)
    act = gate_acc / (1.0 + jnp.exp(-gate_acc))
    activated[...] = act.astype(bf16)
    up_acc = dot(x, up[...], 1, 0) + adapter_scale * dot(low, adapter_part[...], 1, 0)
    value = (act * up_acc).astype(bf16)
    hidden[...] = value
    slot_logits[...] = dot(tag_down[...], value, 1, 1)


def forward(place, own, other, gates, ups, adapter_in, adapter_part, tag_down, rows):
    groups, experts = len(gates), len(own)
    block_rows, share = own[0].shape
    depth, width = gates[0].shape
    per_block = block_rows // rows
    slots = experts * block_rows
    tags, rank = tag_down.shape[0], adapter_in.shape[0]
    whole = lambda array: pl.BlockSpec(array.shape, lambda i, place: (0, 0))
    anywhere = pl.BlockSpec(memory_space=pl.ANY)
    return pl.pallas_call(
        functools.partial(forward_kernel, groups, experts, per_block),
        out_shape=(
            jax.ShapeDtypeStruct((slots, width), bf16),
            jax.ShapeDtypeStruct((slots, width), bf16),
            jax.ShapeDtypeStruct((slots, rank), bf16),
            jax.ShapeDtypeStruct((tags, slots), f32),
        ),
        grid_spec=pltpu.PrefetchScalarGridSpec(
            num_scalar_prefetch=1,
            grid=(slots // rows,),
            in_specs=[anywhere] * (2 * experts + 2 * groups)
            + [whole(adapter_in), whole(adapter_part), whole(tag_down)],
            out_specs=(
                pl.BlockSpec((rows, width), lambda i, place: (i, 0)),
                pl.BlockSpec((rows, width), lambda i, place: (i, 0)),
                pl.BlockSpec((rows, rank), lambda i, place: (i, 0)),
                pl.BlockSpec((tags, rows), lambda i, place: (0, i)),
            ),
            scratch_shapes=[
                pltpu.VMEM((groups * depth, width), bf16),
                pltpu.VMEM((groups * depth, width), bf16),
                pltpu.VMEM((2, rows, 2 * share), bf16),
                pltpu.SemaphoreType.DMA((2, groups)),
                pltpu.SemaphoreType.DMA((2, 2)),
            ],
        ),
        compiler_params=pltpu.CompilerParams(vmem_limit_bytes=vmem_limit),
        cost_estimate=pl.CostEstimate(
            flops=4 * slots * groups * depth * width,
            bytes_accessed=4 * groups * depth * width + 4 * slots * share + 4 * slots * width,
            transcendentals=slots * width,
        ),
        name="gate_up",
    )(place, *own, *other, *gates, *ups, adapter_in, adapter_part, tag_down)


def down_kernel(groups, add, place, hidden, *refs):
    refs = list(refs)
    downs = [refs.pop(0) for _ in range(groups)]
    came = refs.pop(0) if add else None
    weight, sems = refs[-2:]
    outs = refs[:-2]
    step = pl.program_id(0)
    half_count = groups // 2
    width = downs[0].shape[1]
    side = place[1] if add else 1 - place[1]

    @pl.when(step == 0)
    def _():
        for act in ("start", "wait"):
            for k in range(groups):
                _, source = partner(place[0], k, groups)
                column = pl.multiple_of(lax.rem(source, half_count) * width, width)
                copy = pltpu.make_async_copy(downs[k], weight.at[:, pl.ds(column, width)], sems.at[k])
                pl.when(source // half_count == side)(getattr(copy, act))

    value = dot(hidden[...], weight[...], 1, 0)
    if not add:
        outs[0][...] = value.astype(bf16)
        return
    value = (value + came[...].astype(f32)).astype(bf16)
    rows = outs[0].shape[0]
    per_step = value.shape[0] // rows
    for piece in range(groups):
        at = piece % per_step

        @pl.when(step == piece // per_step)
        def _():
            outs[piece][...] = value[at * rows : (at + 1) * rows]


def down(place, hidden, block, block_rows, rows, downs, came, capacity):
    groups = len(downs)
    width, part = downs[0].shape
    share = part * groups // 2
    per_block = block_rows // rows
    add = came is not None
    anywhere = pl.BlockSpec(memory_space=pl.ANY)
    if add:
        out_shape = [jax.ShapeDtypeStruct((capacity, share), bf16)] * groups
        out_specs = [pl.BlockSpec((capacity, share), lambda i, place: (0, 0))] * groups
    else:
        out_shape = jax.ShapeDtypeStruct((block_rows, share), bf16)
        out_specs = pl.BlockSpec((rows, share), lambda i, place: (i, 0))
    in_specs = [pl.BlockSpec((rows, width), lambda i, place: (block * per_block + i, 0))]
    in_specs += [anywhere] * groups
    if add:
        in_specs.append(pl.BlockSpec((rows, share), lambda i, place: (i, 0)))
    return pl.pallas_call(
        functools.partial(down_kernel, groups, add),
        out_shape=out_shape,
        grid_spec=pltpu.PrefetchScalarGridSpec(
            num_scalar_prefetch=1,
            grid=(per_block,),
            in_specs=in_specs,
            out_specs=out_specs,
            scratch_shapes=[pltpu.VMEM((width, share), bf16), pltpu.SemaphoreType.DMA((groups,))],
        ),
        compiler_params=pltpu.CompilerParams(vmem_limit_bytes=vmem_limit),
        cost_estimate=pl.CostEstimate(
            flops=2 * block_rows * width * share,
            bytes_accessed=2 * (block_rows * width + width * share + 2 * block_rows * share),
            transcendentals=0,
        ),
        name="down_own" if add else "down_other",
    )(place, hidden, *downs, *([came] if add else []))


def backward_kernel(experts, per_block, place, *refs):
    refs = list(refs)
    own = [refs.pop(0) for _ in range(experts)]
    other = [refs.pop(0) for _ in range(experts)]
    slot_grad, tag_down, activated, low_rank, adapter_part, out_grad, in_grad, x_scratch, x_sems = refs
    step, steps = pl.program_id(0), pl.num_programs(0)

    @pl.when(step == 0)
    def _():
        row_copies(place, own, other, x_scratch, x_sems, step, per_block, True)
        out_grad[...] = jnp.zeros_like(out_grad)
        in_grad[...] = jnp.zeros_like(in_grad)

    @pl.when(step + 1 < steps)
    def _():
        row_copies(place, own, other, x_scratch, x_sems, step + 1, per_block, True)

    hidden_grad = dot(slot_grad[...], tag_down[...], 0, 0)
    up_grad = (hidden_grad * activated[...].astype(f32)).astype(bf16)
    out_grad[...] += adapter_scale * dot(low_rank[...], up_grad, 0, 0)
    low_grad = (adapter_scale * dot(adapter_part[...], up_grad, 1, 1)).astype(bf16)
    row_copies(place, own, other, x_scratch, x_sems, step, per_block, False)
    in_grad[...] += dot(low_grad, x_scratch[lax.rem(step, 2)], 1, 0)


def backward(place, own, other, slot_grad, tag_down, activated, low_rank, adapter_part, rows):
    experts = len(own)
    block_rows, share = own[0].shape
    per_block = block_rows // rows
    tags, width = tag_down.shape
    slots, rank = low_rank.shape
    whole = lambda shape: pl.BlockSpec(shape, lambda i, place: (0, 0))
    anywhere = pl.BlockSpec(memory_space=pl.ANY)
    return pl.pallas_call(
        functools.partial(backward_kernel, experts, per_block),
        out_shape=(
            jax.ShapeDtypeStruct((rank, width), f32),
            jax.ShapeDtypeStruct((rank, 2 * share), f32),
        ),
        grid_spec=pltpu.PrefetchScalarGridSpec(
            num_scalar_prefetch=1,
            grid=(slots // rows,),
            in_specs=[anywhere] * (2 * experts)
            + [
                pl.BlockSpec((tags, rows), lambda i, place: (0, i)),
                whole(tag_down.shape),
                pl.BlockSpec((rows, width), lambda i, place: (i, 0)),
                pl.BlockSpec((rows, rank), lambda i, place: (i, 0)),
                whole(adapter_part.shape),
            ],
            out_specs=(whole((rank, width)), whole((rank, 2 * share))),
            scratch_shapes=[pltpu.VMEM((2, rows, 2 * share), bf16), pltpu.SemaphoreType.DMA((2, 2))],
        ),
        compiler_params=pltpu.CompilerParams(vmem_limit_bytes=vmem_limit),
        cost_estimate=pl.CostEstimate(
            flops=2 * slots * width * (tags + 2 * rank) + 4 * slots * share * rank,
            bytes_accessed=2 * slots * (width + 2 * share),
            transcendentals=0,
        ),
        name="adapter_grad",
    )(place, *own, *other, slot_grad, tag_down, activated, low_rank, adapter_part)


def local(
    tokens,
    expert_ids,
    gate_values,
    tag_labels,
    w_gate,
    w_up,
    w_down,
    adapter_in,
    adapter_out,
    tag_weight,
):
    experts = lax.axis_size("expert")
    groups = lax.axis_size("dp")
    dp, expert, tensor = lax.axis_index("dp"), lax.axis_index("expert"), lax.axis_index("tensor")
    place = jnp.stack([dp, tensor]).astype(jnp.int32)
    tok_count, model_width = tokens.shape
    share_width = model_width // lax.axis_size("tensor")
    capacity = 3 * tok_count // experts
    feature_part = w_gate.shape[1]
    hidden_part = w_gate.shape[2] // groups
    tags = tag_weight.shape[1]
    rank = adapter_in.shape[1]
    block_rows = groups * capacity
    rows = 4 * capacity

    member = expert_ids[None, :, :] == jnp.arange(experts, dtype=jnp.int32)[:, None, None]
    used = jnp.any(member, axis=2).astype(f32)
    weight = jnp.sum(jnp.where(member, gate_values[None], f32(0.0)), axis=2)
    upto = (jnp.arange(tok_count)[:, None] <= jnp.arange(tok_count)[None, :]).astype(f32)
    code = used * dot(used, upto, 1, 0)
    places = jnp.arange(1, capacity + 1, dtype=f32)
    order = jnp.stack([partner(expert, j, experts)[1] for j in range(experts)])
    ordered_code, ordered_weight = code[order], weight[order]
    own_match = ordered_code[:, None, :] == places[None, :, None]
    combine = jnp.where(own_match, ordered_weight[:, None, :], f32(0.0)).reshape(experts * capacity, tok_count)

    token_half = lax.dynamic_slice_in_dim(tokens, tensor * share_width, share_width, 1)
    plane_tokens = gather(token_half, "dp")
    code_rows = jnp.pad(code, ((0, 8 - experts), (0, 0)))
    plane_code = jnp.stack(gather(code_rows, "dp"))
    plane_tokens = jnp.stack(plane_tokens)
    x_own = []
    for j in range(experts):
        target, _ = partner(expert, j, experts)
        target_code = lax.dynamic_index_in_dim(plane_code, target, 1, keepdims=False)
        match = (target_code[:, None, :] == places[None, :, None]).astype(bf16)
        outgoing = jnp.einsum("gst,gtd->gsd", match, plane_tokens, preferred_element_type=f32).astype(bf16)
        outgoing = outgoing.reshape(block_rows, share_width)
        x_own.append(send(outgoing, "expert", j) if j else outgoing)
    x_other = [send(value, "tensor", 1) for value in x_own]

    tag_part = lax.dynamic_slice_in_dim(tag_weight, dp * feature_part, feature_part, 0)
    tag_down = dot(tag_part, w_down[0], 0, 1).astype(bf16)

    def spread(array, dim, size):
        pieces = []
        for k in range(groups):
            target, _ = partner(dp, k, groups)
            piece = lax.dynamic_slice_in_dim(array, target * size, size, dim)
            pieces.append(send(piece, "dp", k) if k else piece)
        return pieces

    tag_down = total(spread(tag_down, 1, hidden_part)).astype(bf16)
    gates = spread(w_gate[0], 1, hidden_part)
    ups = spread(w_up[0], 1, hidden_part)
    downs = spread(w_down[0], 0, hidden_part)
    adapter_part = lax.dynamic_slice_in_dim(adapter_out[0], dp * hidden_part, hidden_part, 1)

    hidden, activated, low_rank, slot_logits = forward(
        place, x_own, x_other, gates, ups, adapter_in[0], adapter_part, tag_down, rows
    )

    slot_logits = slot_logits + send(slot_logits.astype(bf16), "tensor", 1).astype(f32)
    slot_logits = slot_logits.reshape(tags, experts, groups, capacity).astype(bf16)
    pieces = [slot_logits[:, j] for j in range(experts)]
    pieces = [pieces[0]] + [send(pieces[j], "expert", j) for j in range(1, experts)]
    pieces = jnp.stack(pieces, axis=1)
    pieces = [pieces[:, :, k].reshape(tags, experts * capacity) for k in range(groups)]
    slot_logits = total([pieces[0]] + [send(pieces[k], "dp", k) for k in range(1, groups)])
    logits = dot(tag_weight, tokens, 0, 1) + dot(slot_logits, combine, 1, 0, precision=highest)
    exp_logits = jnp.exp(logits)
    probability = exp_logits / jnp.sum(exp_logits, axis=0, keepdims=True)
    labels_hot = (tag_labels[None, :] == jnp.arange(tags, dtype=jnp.int32)[:, None]).astype(f32)
    logit_grad = probability - labels_hot
    slot_grad = dot(logit_grad, combine, 1, 1, precision=highest).astype(bf16)
    slot_grad = slot_grad.reshape(tags, experts, capacity)
    slot_grad = [slot_grad[:, 0]] + [send(slot_grad[:, j], "expert", j) for j in range(1, experts)]
    slot_grad = gather(jnp.stack(slot_grad, axis=1).reshape(tags, experts * capacity), "dp")
    slot_grad = jnp.stack([value.reshape(tags, experts, capacity) for value in slot_grad], axis=2)
    slot_grad = slot_grad.reshape(tags, experts * block_rows)

    out_local, in_local = backward(
        place, x_own, x_other, slot_grad, tag_down, activated, low_rank, adapter_part, rows
    )
    in_local = in_local + send(in_local.astype(bf16), "tensor", 1).astype(f32)
    in_total = total(gather(in_local.astype(bf16), "dp"))
    out_total = jnp.zeros((rank, groups * hidden_part), f32)
    for k, value in enumerate(gather(out_local, "dp")):
        _, source = partner(dp, k, groups)
        out_total = lax.dynamic_update_slice_in_dim(out_total, value, source * hidden_part, 1)

    returned = [None] * experts
    for j in range(experts - 1, -1, -1):
        other = down(place, hidden, j, block_rows, rows, downs, None, capacity)
        pieces = down(place, hidden, j, block_rows, rows, downs, send(other, "tensor", 1), capacity)
        came = total([pieces[0]] + [send(pieces[k], "dp", k) for k in range(1, groups)]).astype(bf16)
        returned[j] = send(came, "expert", j) if j else came
    returned = jnp.concatenate(returned, axis=0)
    layer_out = token_half.astype(f32) + dot(combine, returned.astype(f32), 0, 0, precision=highest)
    return (layer_out.astype(bf16), in_total[None], out_total[None])


def solution(mesh):
    in_specs = (
        P(("dp", "expert"), None),
        P(("dp", "expert"), None),
        P(("dp", "expert"), None),
        P(("dp", "expert")),
        P("expert", "dp", "tensor"),
        P("expert", "dp", "tensor"),
        P("expert", "tensor", "dp"),
        P("expert", None, None),
        P("expert", None, "tensor"),
        P(),
    )
    out_specs = (
        P(("dp", "expert"), "tensor"),
        P("expert", None, None),
        P("expert", None, "tensor"),
    )
    return jax.shard_map(local, mesh=mesh, in_specs=in_specs, out_specs=out_specs, check_vma=False)
```

```python
import functools

import jax
import jax.numpy as jnp
from jax import lax
from jax.experimental import pallas as pl
from jax.experimental.pallas import tpu as pltpu
from jax.sharding import PartitionSpec as P

adapter_scale = 2.0
f32 = jnp.float32
bf16 = jnp.bfloat16
highest = lax.Precision.HIGHEST
vmem_limit = 50 * 1024 * 1024
lanes = 128


def send(value, axis, step):
    return lax.ppermute(value, axis, [(i, i ^ step) for i in range(lax.axis_size(axis))])


def gather(value, axis):
    return [value] + [send(value, axis, step) for step in range(1, lax.axis_size(axis))]


def swap(values, axis):
    return [values[0]] + [send(values[step], axis, step) for step in range(1, len(values))]


def after(value, *others):
    return lax.optimization_barrier((value, *others))[0]


def total(values):
    result = values[0].astype(f32)
    for value in values[1:]:
        result = result + value.astype(f32)
    return result


def dot(left, right, left_dim, right_dim, **options):
    return lax.dot_general(
        left, right, (((left_dim,), (right_dim,)), ((), ())), preferred_element_type=f32, **options
    )


def row_copies(place, own, other, scratch, sems, step, per_block):
    rows, width = scratch.shape[1], own[0].shape[1]
    slot = lax.rem(step, 2)
    first = pl.multiple_of(lax.rem(step, per_block) * rows, rows)

    def both(block):
        return [
            pltpu.make_async_copy(
                ref.at[pl.ds(first, rows)],
                scratch.at[slot, :, pl.ds(pl.multiple_of(side * width, width), width)],
                sems.at[slot, half],
            )
            for half, (ref, side) in enumerate(((own[block], place[1]), (other[block], 1 - place[1])))
        ]

    return [both(block) for block in range(len(own))]


def start_rows(place, own, other, scratch, sems, step, per_block):
    for block, copies in enumerate(row_copies(place, own, other, scratch, sems, step, per_block)):
        pl.when(step // per_block == block)(functools.partial(start, copies))


def wait_rows(place, own, other, scratch, sems, step, per_block):
    wait(row_copies(place, own, other, scratch, sems, step, per_block)[0])


def start(copies):
    for copy in copies:
        copy.start()


def wait(copies):
    for copy in copies:
        copy.wait()


def low_kernel(experts, per_block, place, *refs):
    own, other, refs = refs[:experts], refs[experts : 2 * experts], refs[2 * experts :]
    adapter_in, out, x_scratch, x_sems = refs
    step, steps = pl.program_id(0), pl.num_programs(0)
    pl.when(step == 0)(lambda: start_rows(place, own, other, x_scratch, x_sems, step, per_block))
    pl.when(step + 1 < steps)(lambda: start_rows(place, own, other, x_scratch, x_sems, step + 1, per_block))
    wait_rows(place, own, other, x_scratch, x_sems, step, per_block)
    out[...] = dot(x_scratch[lax.rem(step, 2)], adapter_in[...], 1, 1).astype(bf16)


def low(place, own, other, adapter_in, rows):
    experts = len(own)
    block_rows, share = own[0].shape
    rank = adapter_in.shape[0]
    return pl.pallas_call(
        functools.partial(low_kernel, experts, block_rows // rows),
        out_shape=jax.ShapeDtypeStruct((experts * block_rows, rank), bf16),
        grid_spec=pltpu.PrefetchScalarGridSpec(
            num_scalar_prefetch=1,
            grid=(experts * block_rows // rows,),
            in_specs=[pl.BlockSpec(memory_space=pl.ANY)] * (2 * experts)
            + [pl.BlockSpec(adapter_in.shape, lambda i, place: (0, 0))],
            out_specs=pl.BlockSpec((rows, rank), lambda i, place: (i, 0)),
            scratch_shapes=[pltpu.VMEM((2, rows, 2 * share), bf16), pltpu.SemaphoreType.DMA((2, 2))],
        ),
        compiler_params=pltpu.CompilerParams(vmem_limit_bytes=vmem_limit),
        name="low_rank",
    )(place, *own, *other, adapter_in)


def forward_kernel(experts, per_block, capacity, place, *refs):
    own, other, refs = refs[:experts], refs[experts : 2 * experts], refs[2 * experts :]
    low_rank, adapter_part, parts, refs = refs[0], refs[1], refs[2], refs[3:]
    groups = parts.shape[0]
    hidden, activated, slot_logits, tag_down = refs[:4]
    weight, tag_parts, x_scratch, added, weight_sems, tag_sems, x_sems = refs[4:]
    step, steps = pl.program_id(0), pl.num_programs(0)
    chunks, depth, pair = weight.shape[0], weight.shape[1] // groups, weight.shape[2]
    width, half = pair // 2, tag_parts.shape[2]
    copy = pltpu.make_async_copy

    def weight_copies(chunk):
        for k in range(groups):
            source = parts.at[k, chunk, pl.ds(0, depth)]
            yield copy(source, weight.at[chunk, pl.ds(k * depth, depth)], weight_sems.at[k, chunk])

    def tag_copies():
        for k in range(groups):
            yield copy(parts.at[k, :, pl.ds(depth, half)], tag_parts.at[k], tag_sems.at[k])

    def work(first):
        x = x_scratch[lax.rem(step, 2)]
        added[...] = adapter_scale * dot(low_rank[...], adapter_part[...], 1, 0)
        for chunk in range(chunks):
            if first:
                wait(weight_copies(chunk))
            columns = slice(chunk * width, (chunk + 1) * width)
            both = dot(x, weight[chunk], 1, 0)
            gate_acc = both[:, :width]
            act = gate_acc / (1.0 + jnp.exp(-gate_acc))
            activated[:, columns] = act.astype(bf16)
            hidden[:, columns] = (act * (both[:, width:] + added[:, columns])).astype(bf16)
        if first:
            wait(tag_copies())
            summed = jnp.sum(tag_parts[...].astype(f32), axis=0).astype(bf16)
            for chunk in range(chunks):
                columns = slice(chunk * width, (chunk + 1) * width)
                tag_down[:half, columns] = summed[chunk, :, :width]
                tag_down[half:, columns] = summed[chunk, :, width:]
        slot_logits[...] = jnp.zeros_like(slot_logits)
        logits = dot(tag_down[...], hidden[...], 1, 1).astype(bf16)
        for piece in range(x.shape[0] // capacity):
            slot_logits[:, piece * lanes : piece * lanes + capacity] = logits[
                :, piece * capacity : (piece + 1) * capacity
            ]

    @pl.when(step == 0)
    def _():
        start_rows(place, own, other, x_scratch, x_sems, step, per_block)
        for chunk in range(chunks):
            start(weight_copies(chunk))
        start(tag_copies())

    @pl.when(step + 1 < steps)
    def _():
        start_rows(place, own, other, x_scratch, x_sems, step + 1, per_block)

    wait_rows(place, own, other, x_scratch, x_sems, step, per_block)
    pl.when(step == 0)(lambda: work(True))
    pl.when(step > 0)(lambda: work(False))


def forward(place, own, other, parts, low_rank, adapter_part, tags, rows, capacity):
    groups, chunks, part_rows, pair = parts.shape
    width, depth = chunks * pair // 2, part_rows - tags // 2
    experts = len(own)
    block_rows, share = own[0].shape
    slots = experts * block_rows
    rank = low_rank.shape[1]
    wide = rows // capacity * lanes
    whole = lambda array: pl.BlockSpec(array.shape, lambda i, place: (0, 0))
    anywhere = pl.BlockSpec(memory_space=pl.ANY)
    return pl.pallas_call(
        functools.partial(forward_kernel, experts, block_rows // rows, capacity),
        out_shape=(
            jax.ShapeDtypeStruct((slots, width), bf16),
            jax.ShapeDtypeStruct((slots, width), bf16),
            jax.ShapeDtypeStruct((tags, slots // capacity * lanes), bf16),
            jax.ShapeDtypeStruct((tags, width), bf16),
        ),
        grid_spec=pltpu.PrefetchScalarGridSpec(
            num_scalar_prefetch=1,
            grid=(slots // rows,),
            in_specs=[anywhere] * (2 * experts)
            + [pl.BlockSpec((rows, rank), lambda i, place: (i, 0)), whole(adapter_part), anywhere],
            out_specs=(
                pl.BlockSpec((rows, width), lambda i, place: (i, 0)),
                pl.BlockSpec((rows, width), lambda i, place: (i, 0)),
                pl.BlockSpec((tags, wide), lambda i, place: (0, i)),
                pl.BlockSpec((tags, width), lambda i, place: (0, 0)),
            ),
            scratch_shapes=[
                pltpu.VMEM((chunks, groups * depth, pair), bf16),
                pltpu.VMEM((groups, chunks, tags // 2, pair), bf16),
                pltpu.VMEM((2, rows, 2 * share), bf16),
                pltpu.VMEM((rows, width), f32),
                pltpu.SemaphoreType.DMA((groups, chunks)),
                pltpu.SemaphoreType.DMA((groups,)),
                pltpu.SemaphoreType.DMA((2, 2)),
            ],
        ),
        compiler_params=pltpu.CompilerParams(vmem_limit_bytes=vmem_limit),
        name="gate_up",
    )(place, *own, *other, low_rank, adapter_part, parts)


def tag_kernel(pieces, *refs):
    parts, (token_logits, combine, labels, slot_grad) = refs[:pieces], refs[pieces:]
    slot_logits = total([part[...] for part in parts])
    logits = token_logits[...] + dot(slot_logits, combine[...], 1, 0, precision=highest)
    exp_logits = jnp.exp(logits)
    probability = exp_logits / jnp.sum(exp_logits, axis=0, keepdims=True)
    hot = labels[...] == lax.broadcasted_iota(jnp.int32, logits.shape, 0)
    logit_grad = probability - jnp.where(hot, f32(1.0), f32(0.0))
    slot_grad[...] = dot(logit_grad, combine[...], 1, 1, precision=highest).astype(bf16)


def fetch_down(groups, place, downs, weight, sems, side):
    half, width = groups // 2, weight.shape[1] // (groups // 2)
    for act in ("start", "wait"):
        for k in range(groups):
            source = place[0] ^ k
            column = pl.multiple_of(lax.rem(source, half) * width, width)
            copy = pltpu.make_async_copy(downs[k], weight.at[:, pl.ds(column, width)], sems.at[k])
            pl.when(source // half == side)(getattr(copy, act))


def other_kernel(groups, place, hidden, *refs):
    downs, (out, weight, sems) = refs[:-3], refs[-3:]
    pl.when(pl.program_id(0) == 0)(lambda: fetch_down(groups, place, downs, weight, sems, 1 - place[1]))
    out[...] = dot(hidden[...], weight[...], 1, 0).astype(bf16)


def own_kernel(groups, capacity, place, hidden, *refs):
    downs, (came, out, weight, sems) = refs[:-4], refs[-4:]
    step = pl.program_id(0)
    pl.when(step == 0)(lambda: fetch_down(groups, place, downs, weight, sems, place[1]))
    value = (dot(hidden[...], weight[...], 1, 0) + came[...].astype(f32)).astype(bf16)
    per_step = value.shape[0] // capacity
    for piece in range(out.shape[1] // capacity * groups):
        block, k = divmod(piece, groups)
        at = piece % per_step

        @pl.when(step == piece // per_step)
        def _():
            out[place[0] ^ k, block * capacity : (block + 1) * capacity] = value[
                at * capacity : (at + 1) * capacity
            ]


def down(place, hidden, groups, first, count, rows, downs, came, capacity):
    width, part = downs[0].shape[-2:]
    share = part * groups // 2
    if came is None:
        out_shape = jax.ShapeDtypeStruct((count, share), bf16)
        out_specs = pl.BlockSpec((rows, share), lambda i, place: (i, 0))
        kernel = functools.partial(other_kernel, groups)
    else:
        out_shape = jax.ShapeDtypeStruct((groups, count // groups, share), bf16)
        out_specs = pl.BlockSpec((groups, count // groups, share), lambda i, place: (0, 0, 0))
        kernel = functools.partial(own_kernel, groups, capacity)
    return pl.pallas_call(
        kernel,
        out_shape=out_shape,
        grid_spec=pltpu.PrefetchScalarGridSpec(
            num_scalar_prefetch=1,
            grid=(count // rows,),
            in_specs=[pl.BlockSpec((rows, width), lambda i, place: (first // rows + i, 0))]
            + [pl.BlockSpec(memory_space=pl.ANY)] * len(downs)
            + ([] if came is None else [pl.BlockSpec((rows, share), lambda i, place: (i, 0))]),
            out_specs=out_specs,
            scratch_shapes=[pltpu.VMEM((width, share), bf16), pltpu.SemaphoreType.DMA((groups,))],
        ),
        compiler_params=pltpu.CompilerParams(vmem_limit_bytes=vmem_limit),
        name="down_other" if came is None else "down_own",
    )(place, hidden, *downs, *([] if came is None else [came]))


def pack_kernel(place, gate, up, down, tag_part, out):
    depth, width = gate.shape
    product = dot(tag_part[...], down[...], 0, 1).astype(bf16)
    half = product.shape[0] // 2
    for chunk in range(width // lanes):
        columns = slice(chunk * lanes, (chunk + 1) * lanes)
        out[0, chunk, :depth, :lanes] = gate[:, columns]
        out[0, chunk, :depth, lanes:] = up[:, columns]
        out[0, chunk, depth:, :lanes] = product[:half, columns]
        out[0, chunk, depth:, lanes:] = product[half:, columns]


def pack(place, gate, up, down, tag_weight, groups):
    depth, width = gate.shape
    part, tags = width // groups, tag_weight.shape[1]
    if part % lanes:
        tag_part = lax.dynamic_slice_in_dim(tag_weight, place[0] * depth, depth, 0)
        product = dot(tag_part, down, 0, 1).astype(bf16)
        rows = [jnp.concatenate([gate, product[: tags // 2]]), jnp.concatenate([up, product[tags // 2 :]])]
        rows = jnp.stack(rows).reshape(2, depth + tags // 2, groups, part)
        return rows.transpose(2, 1, 0, 3).reshape(groups, 1, depth + tags // 2, 2 * part)
    return pl.pallas_call(
        pack_kernel,
        out_shape=jax.ShapeDtypeStruct((groups, part // lanes, depth + tags // 2, 2 * lanes), bf16),
        grid_spec=pltpu.PrefetchScalarGridSpec(
            num_scalar_prefetch=1,
            grid=(groups,),
            in_specs=[
                pl.BlockSpec((depth, part), lambda i, place: (0, i)),
                pl.BlockSpec((depth, part), lambda i, place: (0, i)),
                pl.BlockSpec((part, depth), lambda i, place: (i, 0)),
                pl.BlockSpec((depth, tags), lambda i, place: (place[0], 0)),
            ],
            out_specs=pl.BlockSpec((1, part // lanes, depth + tags // 2, 2 * lanes), lambda i, place: (i, 0, 0, 0)),
        ),
        compiler_params=pltpu.CompilerParams(vmem_limit_bytes=vmem_limit),
        name="pack",
    )(place, gate, up, down, tag_weight)


def backward_kernel(experts, per_block, capacity, place, *refs):
    own, other, refs = refs[:experts], refs[experts : 2 * experts], refs[2 * experts :]
    *slot_grad, tag_down, activated, low_rank, adapter_part, out_grad, in_grad, grads, x_scratch, x_sems = refs
    step, steps = pl.program_id(0), pl.num_programs(0)

    @pl.when(step == 0)
    def _():
        start_rows(place, own, other, x_scratch, x_sems, step, per_block)
        out_grad[...] = jnp.zeros_like(out_grad)
        in_grad[...] = jnp.zeros_like(in_grad)

    @pl.when(step + 1 < steps)
    def _():
        start_rows(place, own, other, x_scratch, x_sems, step + 1, per_block)

    pieces = activated.shape[0] // capacity
    for part in range(per_block):

        @pl.when(lax.rem(step, per_block) == part)
        def _():
            for piece in range(pieces):
                grads[piece] = slot_grad[part * pieces + piece][...]

    hidden_grad = jnp.concatenate([dot(grads[piece][:, :capacity], tag_down[...], 0, 0) for piece in range(pieces)])
    up_grad = (hidden_grad * activated[...].astype(f32)).astype(bf16)
    out_grad[...] += adapter_scale * dot(low_rank[...], up_grad, 0, 0)
    low_grad = (adapter_scale * dot(adapter_part[...], up_grad, 1, 1)).astype(bf16)
    wait_rows(place, own, other, x_scratch, x_sems, step, per_block)
    in_grad[...] += dot(low_grad, x_scratch[lax.rem(step, 2)], 1, 0)


def backward(place, own, other, slot_grad, tag_down, activated, low_rank, adapter_part, rows, capacity):
    experts = len(own)
    block_rows, share = own[0].shape
    per_block = block_rows // rows
    tags, width = tag_down.shape
    slots, rank = low_rank.shape
    whole = lambda shape: pl.BlockSpec(shape, lambda i, place: (0, 0))
    anywhere = pl.BlockSpec(memory_space=pl.ANY)
    return pl.pallas_call(
        functools.partial(backward_kernel, experts, per_block, capacity),
        out_shape=(
            jax.ShapeDtypeStruct((rank, width), f32),
            jax.ShapeDtypeStruct((rank, 2 * share), f32),
        ),
        grid_spec=pltpu.PrefetchScalarGridSpec(
            num_scalar_prefetch=1,
            grid=(slots // rows,),
            in_specs=[anywhere] * (2 * experts)
            + [
                *[pl.BlockSpec((tags, lanes), lambda i, place: (0, i // per_block))] * len(slot_grad),
                whole(tag_down.shape),
                pl.BlockSpec((rows, width), lambda i, place: (i, 0)),
                pl.BlockSpec((rows, rank), lambda i, place: (i, 0)),
                whole(adapter_part.shape),
            ],
            out_specs=(whole((rank, width)), whole((rank, 2 * share))),
            scratch_shapes=[
                pltpu.VMEM((rows // capacity, tags, lanes), bf16),
                pltpu.VMEM((2, rows, 2 * share), bf16),
                pltpu.SemaphoreType.DMA((2, 2)),
            ],
        ),
        compiler_params=pltpu.CompilerParams(vmem_limit_bytes=vmem_limit),
        name="adapter_grad",
    )(place, *own, *other, *slot_grad, tag_down, activated, low_rank, adapter_part)


def local(
    tokens,
    expert_ids,
    gate_values,
    tag_labels,
    w_gate,
    w_up,
    w_down,
    adapter_in,
    adapter_out,
    tag_weight,
):
    experts = lax.axis_size("expert")
    groups = lax.axis_size("dp")
    dp, expert, tensor = lax.axis_index("dp"), lax.axis_index("expert"), lax.axis_index("tensor")
    place = jnp.stack([dp, tensor]).astype(jnp.int32)
    tok_count, model_width = tokens.shape
    share_width = model_width // lax.axis_size("tensor")
    capacity = 3 * tok_count // experts
    feature_part = w_gate.shape[1]
    hidden_part = w_gate.shape[2] // groups
    tags = tag_weight.shape[1]
    rank = adapter_in.shape[1]
    block_rows = groups * capacity
    rows = 4 * capacity

    member = expert_ids[None, :, :] == jnp.arange(experts, dtype=jnp.int32)[:, None, None]
    used = jnp.any(member, axis=2).astype(f32)
    weight = jnp.sum(jnp.where(member, gate_values[None], f32(0.0)), axis=2)
    upto = (jnp.arange(tok_count)[:, None] <= jnp.arange(tok_count)[None, :]).astype(f32)
    code = used * dot(used, upto, 1, 0)
    order = jnp.arange(experts, dtype=jnp.int32) ^ expert
    places = jnp.arange(1, lanes + 1, dtype=jnp.int32).astype(f32)
    own_match = code[order][:, None, :] == places[None, :, None]
    combine = jnp.where(own_match, weight[order][:, None, :], f32(0.0)).reshape(experts * lanes, tok_count)

    token_half = lax.dynamic_slice_in_dim(tokens, tensor * share_width, share_width, 1)
    code_rows = jnp.pad(code.astype(bf16), ((0, 8 - experts), (0, share_width - tok_count)))
    plane = gather(jnp.concatenate([token_half, code_rows], axis=0), "dp")
    parts = pack(place, w_gate[0], w_up[0], w_down[0], tag_weight, groups)
    plane_parts = plane
    plane = jnp.stack(plane)
    plane_code = plane[:, tok_count : tok_count + experts, :tok_count].astype(f32)
    plane_tokens = plane[:, :tok_count]
    downs = [lax.dynamic_slice_in_dim(w_down[0], (dp ^ k) * hidden_part, hidden_part, 0) for k in range(groups)]
    plane_tokens = after(plane_tokens, parts, *downs)
    parts = lax.all_to_all(after(parts, *plane_parts), "dp", split_axis=0, concat_axis=0, tiled=True)
    x_own = []
    for j in range(experts):
        target_code = lax.dynamic_index_in_dim(plane_code, expert ^ j, 1, keepdims=False)
        match = (target_code[:, None, :] == places[None, :capacity, None]).astype(bf16)
        outgoing = jnp.einsum("gst,gtd->gsd", match, plane_tokens, preferred_element_type=f32).astype(bf16)
        x_own.append(outgoing.reshape(block_rows, share_width))
    x_own = swap(x_own, "expert")
    x_other = [send(value, "tensor", 1) for value in x_own]
    low_rank = low(place, x_own, x_other, adapter_in[0], rows)
    parts = after(parts, low_rank)
    downs = swap([after(piece, parts) for piece in downs], "dp")
    adapter_part = lax.dynamic_slice_in_dim(adapter_out[0], dp * hidden_part, hidden_part, 1)

    hidden, activated, slot_logits, tag_down = forward(
        place, x_own, x_other, parts, low_rank, adapter_part, tags, rows, capacity
    )

    slot_logits = (slot_logits.astype(f32) + send(slot_logits, "tensor", 1).astype(f32)).astype(bf16)
    plane_lanes = groups * lanes
    pieces = [slot_logits[:, j * plane_lanes : (j + 1) * plane_lanes] for j in range(experts)]
    pieces = swap(pieces, "expert")

    chunks = [(experts // 2, experts // 2), (0, experts // 2)]

    def product(chunk, came):
        first, count = chunks[chunk]
        return down(place, hidden, groups, first * block_rows, count * block_rows, rows, downs, came, capacity)

    hidden = after(hidden, *pieces)
    others, mine = [], []
    for chunk in range(len(chunks)):
        others.append(send(product(chunk, None), "tensor", 1))
        mine.append(product(chunk, others[chunk]))
        hidden = after(hidden, mine[chunk])
    came = [lax.all_to_all(part, "dp", split_axis=0, concat_axis=0, tiled=True) for part in mine]
    pieces = [
        jnp.concatenate([piece[:, k * lanes : (k + 1) * lanes] for piece in pieces], axis=1) for k in range(groups)
    ]
    pieces = swap(pieces, "dp")
    slot_grad = pl.pallas_call(
        functools.partial(tag_kernel, groups),
        out_shape=jax.ShapeDtypeStruct((tags, experts * lanes), bf16),
        compiler_params=pltpu.CompilerParams(vmem_limit_bytes=vmem_limit),
        name="tag_grad",
    )(*pieces, dot(tag_weight, tokens, 0, 1), combine, tag_labels[None, :])
    slot_grad = after(slot_grad, mine[-1])
    slot_grad = swap([slot_grad[:, j * lanes : (j + 1) * lanes] for j in range(experts)], "expert")
    slot_grad = gather(jnp.concatenate(slot_grad, axis=1), "dp")

    tag_down = after(tag_down, came[0])
    out_local, in_local = backward(
        place, x_own, x_other, slot_grad, tag_down, activated, low_rank, adapter_part, rows, capacity
    )
    in_local = in_local + send(in_local.astype(bf16), "tensor", 1).astype(f32)
    both = gather(jnp.concatenate([in_local, out_local], axis=1).astype(bf16), "dp")
    in_total = total([value[:, :model_width] for value in both])
    out_total = jnp.zeros((rank, groups * hidden_part), f32)
    for k, value in enumerate(both):
        out_total = lax.dynamic_update_slice_in_dim(
            out_total, value[:, model_width:].astype(f32), (dp ^ k) * hidden_part, 1
        )

    returned = [None] * experts
    for (first, count), value in zip(chunks, came):
        if first == 0:
            value = after(value, *returned[count:])
        value = jnp.sum(value.astype(f32), axis=0).astype(bf16)
        for j in range(first, first + count):
            kept = value[(j - first) * capacity : (j - first + 1) * capacity]
            returned[j] = send(kept, "expert", j) if j else kept
    layer_out = token_half.astype(f32)
    for j in range(experts):
        kept = combine[j * lanes : j * lanes + capacity]
        layer_out = layer_out + dot(kept, returned[j].astype(f32), 0, 0, precision=highest)
    layer_out = layer_out.astype(bf16)
    return (layer_out, in_total[None], out_total[None])


def solution(mesh):
    in_specs = (
        P(("dp", "expert"), None),
        P(("dp", "expert"), None),
        P(("dp", "expert"), None),
        P(("dp", "expert")),
        P("expert", "dp", "tensor"),
        P("expert", "dp", "tensor"),
        P("expert", "tensor", "dp"),
        P("expert", None, None),
        P("expert", None, "tensor"),
        P(),
    )
    out_specs = (
        P(("dp", "expert"), "tensor"),
        P("expert", None, None),
        P("expert", None, "tensor"),
    )
    return jax.shard_map(local, mesh=mesh, in_specs=in_specs, out_specs=out_specs, check_vma=False)
```

```python
import functools

import jax
import jax.numpy as jnp
from jax import lax
from jax.experimental import pallas as pl
from jax.experimental.pallas import tpu as pltpu
from jax.sharding import PartitionSpec as P

adapter_scale = 2.0
f32 = jnp.float32
bf16 = jnp.bfloat16
highest = lax.Precision.HIGHEST
vmem_limit = 52 * 1024 * 1024
lanes = 128


def send(value, axis, step):
    return lax.ppermute(value, axis, [(i, i ^ step) for i in range(lax.axis_size(axis))])


def gather(value, axis):
    return [value] + [send(value, axis, step) for step in range(1, lax.axis_size(axis))]


def swap(values, axis):
    return [values[0]] + [send(values[step], axis, step) for step in range(1, len(values))]


def after(value, *others):
    return lax.optimization_barrier((value, *others))[0]


def total(values):
    result = values[0].astype(f32)
    for value in values[1:]:
        result = result + value.astype(f32)
    return result


def dot(left, right, left_dim, right_dim, **options):
    return lax.dot_general(
        left, right, (((left_dim,), (right_dim,)), ((), ())), preferred_element_type=f32, **options
    )


def row_copies(place, own, other, scratch, sems, step, per_block):
    rows, width = scratch.shape[1], own[0].shape[1]
    slot = lax.rem(step, 2)
    first = pl.multiple_of(lax.rem(step, per_block) * rows, rows)

    def both(block):
        return [
            pltpu.make_async_copy(
                ref.at[pl.ds(first, rows)],
                scratch.at[slot, :, pl.ds(pl.multiple_of(side * width, width), width)],
                sems.at[slot, half],
            )
            for half, (ref, side) in enumerate(((own[block], place[1]), (other[block], 1 - place[1])))
        ]

    return [both(block) for block in range(len(own))]


def start_rows(place, own, other, scratch, sems, step, per_block):
    for block, copies in enumerate(row_copies(place, own, other, scratch, sems, step, per_block)):
        pl.when(step // per_block == block)(functools.partial(start, copies))


def wait_rows(place, own, other, scratch, sems, step, per_block):
    wait(row_copies(place, own, other, scratch, sems, step, per_block)[0])


def start(copies):
    for copy in copies:
        copy.start()


def wait(copies):
    for copy in copies:
        copy.wait()


def low_kernel(experts, per_block, place, *refs):
    own, other, refs = refs[:experts], refs[experts : 2 * experts], refs[2 * experts :]
    adapter_in, out, x_scratch, x_sems = refs
    step, steps = pl.program_id(0), pl.num_programs(0)
    pl.when(step == 0)(lambda: start_rows(place, own, other, x_scratch, x_sems, step, per_block))
    pl.when(step + 1 < steps)(lambda: start_rows(place, own, other, x_scratch, x_sems, step + 1, per_block))
    wait_rows(place, own, other, x_scratch, x_sems, step, per_block)
    out[...] = dot(x_scratch[lax.rem(step, 2)], adapter_in[...], 1, 1).astype(bf16)


def low(place, own, other, adapter_in, rows):
    experts = len(own)
    block_rows, share = own[0].shape
    rank = adapter_in.shape[0]
    return pl.pallas_call(
        functools.partial(low_kernel, experts, block_rows // rows),
        out_shape=jax.ShapeDtypeStruct((experts * block_rows, rank), bf16),
        grid_spec=pltpu.PrefetchScalarGridSpec(
            num_scalar_prefetch=1,
            grid=(experts * block_rows // rows,),
            in_specs=[pl.BlockSpec(memory_space=pl.ANY)] * (2 * experts)
            + [pl.BlockSpec(adapter_in.shape, lambda i, place: (0, 0))],
            out_specs=pl.BlockSpec((rows, rank), lambda i, place: (i, 0)),
            scratch_shapes=[pltpu.VMEM((2, rows, 2 * share), bf16), pltpu.SemaphoreType.DMA((2, 2))],
        ),
        compiler_params=pltpu.CompilerParams(vmem_limit_bytes=vmem_limit),
        name="low_rank",
    )(place, *own, *other, adapter_in)


def forward_kernel(experts, per_block, capacity, place, *refs):
    own, other, refs = refs[:experts], refs[experts : 2 * experts], refs[2 * experts :]
    low_rank, adapter_part, parts, refs = refs[0], refs[1], refs[2], refs[3:]
    groups = parts.shape[0]
    hidden, activated, slot_logits, tag_down = refs[:4]
    weight, tag_parts, x_scratch, added, weight_sems, tag_sems, x_sems = refs[4:]
    step, steps = pl.program_id(0), pl.num_programs(0)
    chunks, depth, pair = weight.shape[0], weight.shape[1] // groups, weight.shape[2]
    width, half = pair // 2, tag_parts.shape[2]
    copy = pltpu.make_async_copy

    def weight_copies(chunk):
        for k in range(groups):
            source = parts.at[k, chunk, pl.ds(0, depth)]
            yield copy(source, weight.at[chunk, pl.ds(k * depth, depth)], weight_sems.at[k, chunk])

    def tag_copies():
        for k in range(groups):
            yield copy(parts.at[k, :, pl.ds(depth, half)], tag_parts.at[k], tag_sems.at[k])

    @pl.when(step == 0)
    def _():
        start_rows(place, own, other, x_scratch, x_sems, step, per_block)
        for chunk in range(chunks):
            start(weight_copies(chunk))
        start(tag_copies())

    @pl.when(step + 1 < steps)
    def _():
        start_rows(place, own, other, x_scratch, x_sems, step + 1, per_block)

    @pl.when(step == 0)
    def _():
        for chunk in range(chunks):
            wait(weight_copies(chunk))
        wait(tag_copies())
        summed = jnp.sum(tag_parts[...].astype(f32), axis=0).astype(bf16)
        for chunk in range(chunks):
            columns = slice(chunk * width, (chunk + 1) * width)
            tag_down[:half, columns] = summed[chunk, :, :width]
            tag_down[half:, columns] = summed[chunk, :, width:]

    added[...] = adapter_scale * dot(low_rank[...], adapter_part[...], 1, 0)
    wait_rows(place, own, other, x_scratch, x_sems, step, per_block)
    slot = lax.rem(step, 2)
    for chunk in range(chunks):
        columns = slice(chunk * width, (chunk + 1) * width)
        both = dot(x_scratch[slot], weight[chunk], 1, 0)
        gate_acc = both[:, :width]
        act = gate_acc / (1.0 + jnp.exp(-gate_acc))
        activated[:, columns] = act.astype(bf16)
        hidden[:, columns] = (act * (both[:, width:] + added[:, columns])).astype(bf16)
    slot_logits[...] = jnp.zeros_like(slot_logits)
    logits = dot(tag_down[...], hidden[...], 1, 1).astype(bf16)
    for piece in range(logits.shape[1] // capacity):
        slot_logits[:, piece * lanes : piece * lanes + capacity] = logits[
            :, piece * capacity : (piece + 1) * capacity
        ]


def forward(place, own, other, parts, low_rank, adapter_part, tags, rows, capacity):
    groups, chunks, part_rows, pair = parts.shape
    width, depth = chunks * pair // 2, part_rows - tags // 2
    experts = len(own)
    block_rows, share = own[0].shape
    slots = experts * block_rows
    rank = low_rank.shape[1]
    wide = rows // capacity * lanes
    whole = lambda array: pl.BlockSpec(array.shape, lambda i, place: (0, 0))
    anywhere = pl.BlockSpec(memory_space=pl.ANY)
    return pl.pallas_call(
        functools.partial(forward_kernel, experts, block_rows // rows, capacity),
        out_shape=(
            jax.ShapeDtypeStruct((slots, width), bf16),
            jax.ShapeDtypeStruct((slots, width), bf16),
            jax.ShapeDtypeStruct((tags, slots // capacity * lanes), bf16),
            jax.ShapeDtypeStruct((tags, width), bf16),
        ),
        grid_spec=pltpu.PrefetchScalarGridSpec(
            num_scalar_prefetch=1,
            grid=(slots // rows,),
            in_specs=[anywhere] * (2 * experts)
            + [pl.BlockSpec((rows, rank), lambda i, place: (i, 0)), whole(adapter_part), anywhere],
            out_specs=(
                pl.BlockSpec((rows, width), lambda i, place: (i, 0)),
                pl.BlockSpec((rows, width), lambda i, place: (i, 0)),
                pl.BlockSpec((tags, wide), lambda i, place: (0, i)),
                pl.BlockSpec((tags, width), lambda i, place: (0, 0)),
            ),
            scratch_shapes=[
                pltpu.VMEM((chunks, groups * depth, pair), bf16),
                pltpu.VMEM((groups, chunks, tags // 2, pair), bf16),
                pltpu.VMEM((2, rows, 2 * share), bf16),
                pltpu.VMEM((rows, width), f32),
                pltpu.SemaphoreType.DMA((groups, chunks)),
                pltpu.SemaphoreType.DMA((groups,)),
                pltpu.SemaphoreType.DMA((2, 2)),
            ],
        ),
        compiler_params=pltpu.CompilerParams(vmem_limit_bytes=vmem_limit),
        name="gate_up",
    )(place, *own, *other, low_rank, adapter_part, parts)


def tag_kernel(pieces, *refs):
    parts, (token_logits, combine, labels, slot_grad) = refs[:pieces], refs[pieces:]
    slot_logits = total([part[...] for part in parts])
    logits = token_logits[...] + dot(slot_logits, combine[...], 1, 0, precision=highest)
    exp_logits = jnp.exp(logits)
    probability = exp_logits / jnp.sum(exp_logits, axis=0, keepdims=True)
    hot = labels[...] == lax.broadcasted_iota(jnp.int32, logits.shape, 0)
    logit_grad = probability - jnp.where(hot, f32(1.0), f32(0.0))
    slot_grad[...] = dot(logit_grad, combine[...], 1, 1, precision=highest).astype(bf16)


def fetch_down(groups, place, downs, weight, sems, side):
    half, width = groups // 2, weight.shape[1] // (groups // 2)
    for act in ("start", "wait"):
        for k in range(groups):
            source = place[0] ^ k
            column = pl.multiple_of(lax.rem(source, half) * width, width)
            copy = pltpu.make_async_copy(downs[k], weight.at[:, pl.ds(column, width)], sems.at[k])
            pl.when(source // half == side)(getattr(copy, act))


def column_chunks(count):
    size = min(count, 2 * lanes)
    return [slice(at, at + size) for at in range(0, count, size)]


def other_kernel(groups, place, hidden, *refs):
    downs, outs, (weight, sems) = refs[:groups], refs[groups:-2], refs[-2:]
    step, steps = pl.program_id(0), pl.num_programs(0)
    pl.when(step == 0)(lambda: fetch_down(groups, place, downs, weight, sems, 1 - place[1]))
    for out, ref in enumerate(outs):

        @pl.when(step // (steps // len(outs)) == out)
        def _():
            for columns in column_chunks(ref.shape[1]):
                ref[:, columns] = dot(hidden[...], weight[:, columns], 1, 0).astype(bf16)


def own_kernel(groups, capacity, place, hidden, *refs):
    downs, (came, out, weight, sems) = refs[:groups], refs[groups:]
    step = pl.program_id(0)
    pl.when(step == 0)(lambda: fetch_down(groups, place, downs, weight, sems, place[1]))
    per_step = hidden.shape[0] // capacity
    per_block = groups // per_step
    row = pl.ds(pl.multiple_of(step // per_block * capacity, capacity), capacity)
    for columns in column_chunks(out.shape[2]):
        value = (dot(hidden[...], weight[:, columns], 1, 0) + came[:, columns].astype(f32)).astype(bf16)
        for piece in range(per_step):
            k = lax.rem(step, per_block) * per_step + piece
            out[place[0] ^ k, row, columns] = value[piece * capacity : (piece + 1) * capacity]


def chunk_block(first, count, step, place):
    return jnp.clip(step - first, 0, count - 1), 0


def down_other(place, hidden, groups, rows, downs, chunks):
    slots, (width, part) = hidden.shape[0], downs[0].shape
    share = part * groups // 2
    half = slots // chunks // rows
    return pl.pallas_call(
        functools.partial(other_kernel, groups),
        out_shape=[jax.ShapeDtypeStruct((slots // chunks, share), bf16)] * chunks,
        grid_spec=pltpu.PrefetchScalarGridSpec(
            num_scalar_prefetch=1,
            grid=(slots // rows,),
            in_specs=[
                pl.BlockSpec((rows, width), lambda i, place: ((chunks - 1 - i // half) * half + lax.rem(i, half), 0))
            ]
            + [pl.BlockSpec(memory_space=pl.ANY)] * groups,
            out_specs=[
                pl.BlockSpec((rows, share), functools.partial(chunk_block, chunk * half, half)) for chunk in range(chunks)
            ],
            scratch_shapes=[pltpu.VMEM((width, share), bf16), pltpu.SemaphoreType.DMA((groups,))],
        ),
        compiler_params=pltpu.CompilerParams(vmem_limit_bytes=62 * 1024 * 1024),
        name="down_other",
    )(place, hidden, *downs)


def down_own(place, hidden, groups, first, rows, downs, came, capacity):
    count, share = came.shape
    width = hidden.shape[1]
    shape = (groups, count // groups, share)
    return pl.pallas_call(
        functools.partial(own_kernel, groups, capacity),
        out_shape=jax.ShapeDtypeStruct(shape, bf16),
        grid_spec=pltpu.PrefetchScalarGridSpec(
            num_scalar_prefetch=1,
            grid=(count // rows,),
            in_specs=[pl.BlockSpec((rows, width), lambda i, place: (first // rows + i, 0))]
            + [pl.BlockSpec(memory_space=pl.ANY)] * groups
            + [pl.BlockSpec((rows, share), lambda i, place: (i, 0))],
            out_specs=pl.BlockSpec(shape, lambda i, place: (0, 0, 0)),
            scratch_shapes=[pltpu.VMEM((width, share), bf16), pltpu.SemaphoreType.DMA((groups,))],
        ),
        compiler_params=pltpu.CompilerParams(vmem_limit_bytes=62 * 1024 * 1024),
        name="down_own",
    )(place, hidden, *downs, came)


def pack_kernel(place, gate, up, down, tag_part, out):
    depth, width = gate.shape
    product = dot(tag_part[...], down[...], 0, 1).astype(bf16)
    half = product.shape[0] // 2
    for chunk in range(width // lanes):
        columns = slice(chunk * lanes, (chunk + 1) * lanes)
        out[0, chunk, :depth, :lanes] = gate[:, columns]
        out[0, chunk, :depth, lanes:] = up[:, columns]
        out[0, chunk, depth:, :lanes] = product[:half, columns]
        out[0, chunk, depth:, lanes:] = product[half:, columns]


def pack(place, gate, up, down, tag_weight, groups):
    depth, width = gate.shape
    part, tags = width // groups, tag_weight.shape[1]
    if part % lanes:
        tag_part = lax.dynamic_slice_in_dim(tag_weight, place[0] * depth, depth, 0)
        product = dot(tag_part, down, 0, 1).astype(bf16)
        rows = [jnp.concatenate([gate, product[: tags // 2]]), jnp.concatenate([up, product[tags // 2 :]])]
        rows = jnp.stack(rows).reshape(2, depth + tags // 2, groups, part)
        return rows.transpose(2, 1, 0, 3).reshape(groups, 1, depth + tags // 2, 2 * part)
    return pl.pallas_call(
        pack_kernel,
        out_shape=jax.ShapeDtypeStruct((groups, part // lanes, depth + tags // 2, 2 * lanes), bf16),
        grid_spec=pltpu.PrefetchScalarGridSpec(
            num_scalar_prefetch=1,
            grid=(groups,),
            in_specs=[
                pl.BlockSpec((depth, part), lambda i, place: (0, i)),
                pl.BlockSpec((depth, part), lambda i, place: (0, i)),
                pl.BlockSpec((part, depth), lambda i, place: (i, 0)),
                pl.BlockSpec((depth, tags), lambda i, place: (place[0], 0)),
            ],
            out_specs=pl.BlockSpec((1, part // lanes, depth + tags // 2, 2 * lanes), lambda i, place: (i, 0, 0, 0)),
        ),
        compiler_params=pltpu.CompilerParams(vmem_limit_bytes=vmem_limit),
        name="pack",
    )(place, gate, up, down, tag_weight)


def backward_kernel(experts, per_block, capacity, place, *refs):
    own, other, refs = refs[:experts], refs[experts : 2 * experts], refs[2 * experts :]
    *slot_grad, tag_down, activated, low_rank, adapter_part, out_grad, in_grad, grads, x_scratch, x_sems = refs
    step, steps = pl.program_id(0), pl.num_programs(0)

    @pl.when(step == 0)
    def _():
        start_rows(place, own, other, x_scratch, x_sems, step, per_block)
        out_grad[...] = jnp.zeros_like(out_grad)
        in_grad[...] = jnp.zeros_like(in_grad)

    @pl.when(step + 1 < steps)
    def _():
        start_rows(place, own, other, x_scratch, x_sems, step + 1, per_block)

    pieces = activated.shape[0] // capacity
    for part in range(per_block):

        @pl.when(lax.rem(step, per_block) == part)
        def _():
            for piece in range(pieces):
                grads[piece] = slot_grad[part * pieces + piece][...]

    hidden_grad = jnp.concatenate([dot(grads[piece][:, :capacity], tag_down[...], 0, 0) for piece in range(pieces)])
    up_grad = (hidden_grad * activated[...].astype(f32)).astype(bf16)
    out_grad[...] += adapter_scale * dot(low_rank[...], up_grad, 0, 0)
    low_grad = (adapter_scale * dot(adapter_part[...], up_grad, 1, 1)).astype(bf16)
    wait_rows(place, own, other, x_scratch, x_sems, step, per_block)
    in_grad[...] += dot(low_grad, x_scratch[lax.rem(step, 2)], 1, 0)


def backward(place, own, other, slot_grad, tag_down, activated, low_rank, adapter_part, rows, capacity):
    experts = len(own)
    block_rows, share = own[0].shape
    per_block = block_rows // rows
    tags, width = tag_down.shape
    slots, rank = low_rank.shape
    whole = lambda shape: pl.BlockSpec(shape, lambda i, place: (0, 0))
    anywhere = pl.BlockSpec(memory_space=pl.ANY)
    return pl.pallas_call(
        functools.partial(backward_kernel, experts, per_block, capacity),
        out_shape=(
            jax.ShapeDtypeStruct((rank, width), f32),
            jax.ShapeDtypeStruct((rank, 2 * share), f32),
        ),
        grid_spec=pltpu.PrefetchScalarGridSpec(
            num_scalar_prefetch=1,
            grid=(slots // rows,),
            in_specs=[anywhere] * (2 * experts)
            + [
                *[pl.BlockSpec((tags, lanes), lambda i, place: (0, i // per_block))] * len(slot_grad),
                whole(tag_down.shape),
                pl.BlockSpec((rows, width), lambda i, place: (i, 0)),
                pl.BlockSpec((rows, rank), lambda i, place: (i, 0)),
                whole(adapter_part.shape),
            ],
            out_specs=(whole((rank, width)), whole((rank, 2 * share))),
            scratch_shapes=[
                pltpu.VMEM((rows // capacity, tags, lanes), bf16),
                pltpu.VMEM((2, rows, 2 * share), bf16),
                pltpu.SemaphoreType.DMA((2, 2)),
            ],
        ),
        compiler_params=pltpu.CompilerParams(vmem_limit_bytes=vmem_limit),
        name="adapter_grad",
    )(place, *own, *other, *slot_grad, tag_down, activated, low_rank, adapter_part)


def finish_kernel(place, *refs):
    both, (in_total, out_total) = refs[:-2], refs[-2:]
    width = in_total.shape[1]
    in_total[...] = total([ref[:, :width] for ref in both])
    part = both[0].shape[1] - width
    for k, ref in enumerate(both):
        column = pl.multiple_of((place[0] ^ k) * part, part)
        out_total[:, pl.ds(column, part)] = ref[:, width:].astype(f32)


def finish(place, both, width):
    rank, part, groups = both[0].shape[0], both[0].shape[1] - width, len(both)
    if part % lanes:
        out_total = jnp.zeros((rank, groups * part), f32)
        for k, value in enumerate(both):
            value = value[:, width:].astype(f32)
            out_total = lax.dynamic_update_slice_in_dim(out_total, value, (place[0] ^ k) * part, 1)
        return total([value[:, :width] for value in both]), out_total
    whole = lambda shape: pl.BlockSpec(shape, lambda i, place: (0, 0))
    shapes = (rank, width), (rank, groups * part)
    return pl.pallas_call(
        finish_kernel,
        out_shape=[jax.ShapeDtypeStruct(shape, f32) for shape in shapes],
        grid_spec=pltpu.PrefetchScalarGridSpec(
            num_scalar_prefetch=1,
            grid=(1,),
            in_specs=[whole(value.shape) for value in both],
            out_specs=[whole(shape) for shape in shapes],
        ),
        compiler_params=pltpu.CompilerParams(vmem_limit_bytes=vmem_limit),
        name="finish",
    )(place, *both)


def local(
    tokens,
    expert_ids,
    gate_values,
    tag_labels,
    w_gate,
    w_up,
    w_down,
    adapter_in,
    adapter_out,
    tag_weight,
):
    experts = lax.axis_size("expert")
    groups = lax.axis_size("dp")
    dp, expert, tensor = lax.axis_index("dp"), lax.axis_index("expert"), lax.axis_index("tensor")
    place = jnp.stack([dp, tensor]).astype(jnp.int32)
    tok_count, model_width = tokens.shape
    share_width = model_width // lax.axis_size("tensor")
    capacity = 3 * tok_count // experts
    feature_part = w_gate.shape[1]
    hidden_part = w_gate.shape[2] // groups
    tags = tag_weight.shape[1]
    rank = adapter_in.shape[1]
    block_rows = groups * capacity
    rows = 4 * capacity

    member = expert_ids[None, :, :] == jnp.arange(experts, dtype=jnp.int32)[:, None, None]
    used = jnp.any(member, axis=2).astype(f32)
    weight = jnp.sum(jnp.where(member, gate_values[None], f32(0.0)), axis=2)
    upto = (jnp.arange(tok_count)[:, None] <= jnp.arange(tok_count)[None, :]).astype(f32)
    code = used * dot(used, upto, 1, 0)
    order = jnp.arange(experts, dtype=jnp.int32) ^ expert
    places = jnp.arange(1, lanes + 1, dtype=jnp.int32).astype(f32)
    own_match = code[order][:, None, :] == places[None, :, None]
    combine = jnp.where(own_match, weight[order][:, None, :], f32(0.0)).reshape(experts * lanes, tok_count)

    token_half = lax.dynamic_slice_in_dim(tokens, tensor * share_width, share_width, 1)
    code_rows = jnp.pad(code.astype(bf16), ((0, 8 - experts), (0, share_width - tok_count)))
    plane = gather(jnp.concatenate([token_half, code_rows], axis=0), "dp")
    parts = pack(place, w_gate[0], w_up[0], w_down[0], tag_weight, groups)
    plane_parts = plane
    plane = jnp.stack(plane)
    plane_code = plane[:, tok_count : tok_count + experts, :tok_count].astype(f32)
    plane_tokens = plane[:, :tok_count]
    downs = [lax.dynamic_slice_in_dim(w_down[0], (dp ^ k) * hidden_part, hidden_part, 0) for k in range(groups)]
    plane_tokens = after(plane_tokens, parts, *downs)
    parts = lax.all_to_all(after(parts, *plane_parts), "dp", split_axis=0, concat_axis=0, tiled=True)
    x_own = []
    for j in range(experts):
        target_code = lax.dynamic_index_in_dim(plane_code, expert ^ j, 1, keepdims=False)
        match = (target_code[:, None, :] == places[None, :capacity, None]).astype(bf16)
        outgoing = jnp.einsum("gst,gtd->gsd", match, plane_tokens, preferred_element_type=f32).astype(bf16)
        x_own.append(outgoing.reshape(block_rows, share_width))
    x_own = swap(x_own, "expert")
    x_other = [send(value, "tensor", 1) for value in x_own]
    low_rank = low(place, x_own, x_other, adapter_in[0], rows)
    token_logits = dot(tag_weight, tokens, 0, 1)
    parts = after(parts, low_rank, combine, token_logits)
    downs = swap([after(piece, parts) for piece in downs], "dp")
    adapter_part = lax.dynamic_slice_in_dim(adapter_out[0], dp * hidden_part, hidden_part, 1)

    hidden, activated, slot_logits, tag_down = forward(
        place, x_own, x_other, parts, low_rank, adapter_part, tags, rows, capacity
    )

    slot_logits = (slot_logits.astype(f32) + send(slot_logits, "tensor", 1).astype(f32)).astype(bf16)
    plane_lanes = groups * lanes
    pieces = [slot_logits[:, j * plane_lanes : (j + 1) * plane_lanes] for j in range(experts)]
    pieces = swap(pieces, "expert")

    hidden = after(hidden, *pieces)
    pieces = [
        jnp.concatenate([piece[:, k * lanes : (k + 1) * lanes] for piece in pieces], axis=1) for k in range(groups)
    ]
    pieces = swap(pieces, "dp")

    chunks = [(experts // 2, experts // 2), (0, experts // 2)]

    def own(chunk, came):
        return down_own(place, hidden, groups, chunks[chunk][0] * block_rows, rows, downs, came, capacity)

    def change(part):
        return lax.all_to_all(part, "dp", split_axis=0, concat_axis=0, tiled=True)

    others = down_other(place, hidden, groups, rows, downs, len(chunks))
    others = [send(other, "tensor", 1) for other in others]
    first = own(0, after(others[0], *pieces))

    pieces[0] = after(pieces[0], first)
    slot_grad = pl.pallas_call(
        functools.partial(tag_kernel, groups),
        out_shape=jax.ShapeDtypeStruct((tags, experts * lanes), bf16),
        compiler_params=pltpu.CompilerParams(vmem_limit_bytes=vmem_limit),
        name="tag_grad",
    )(*pieces, token_logits, combine, tag_labels[None, :])
    slot_grad = swap([slot_grad[:, j * lanes : (j + 1) * lanes] for j in range(experts)], "expert")
    second = own(1, after(others[1], *slot_grad))
    slot_grad[0] = after(slot_grad[0], second)
    slot_grad = gather(jnp.concatenate(slot_grad, axis=1), "dp")
    came = [change(first), change(after(second, *slot_grad[1:]))]

    sums = [jnp.sum(came[0].astype(f32), axis=0).astype(bf16)]
    slot_grad[0] = after(slot_grad[0], sums[0])
    out_local, in_local = backward(
        place, x_own, x_other, slot_grad, tag_down, activated, low_rank, adapter_part, rows, capacity
    )
    returned = [None] * experts

    def give_back(chunk):
        first, count = chunks[chunk]
        for j in range(first, first + count):
            kept = sums[chunk][(j - first) * capacity : (j - first + 1) * capacity]
            returned[j] = send(kept, "expert", j) if j else kept

    give_back(0)
    in_local = after(in_local, *returned[chunks[0][0] :])
    in_local = in_local + send(in_local.astype(bf16), "tensor", 1).astype(f32)
    both = gather(jnp.concatenate([in_local, out_local], axis=1).astype(bf16), "dp")
    sums.append(jnp.sum(came[1].astype(f32), axis=0).astype(bf16))
    give_back(1)
    both[0] = after(both[0], sums[-1])
    in_total, out_total = finish(place, both, model_width)
    layer_out = token_half.astype(f32)
    for j in range(experts):
        kept = combine[j * lanes : j * lanes + capacity]
        layer_out = layer_out + dot(kept, returned[j].astype(f32), 0, 0, precision=highest)
    layer_out = layer_out.astype(bf16)
    return (layer_out, in_total[None], out_total[None])


def solution(mesh):
    in_specs = (
        P(("dp", "expert"), None),
        P(("dp", "expert"), None),
        P(("dp", "expert"), None),
        P(("dp", "expert")),
        P("expert", "dp", "tensor"),
        P("expert", "dp", "tensor"),
        P("expert", "tensor", "dp"),
        P("expert", None, None),
        P("expert", None, "tensor"),
        P(),
    )
    out_specs = (
        P(("dp", "expert"), "tensor"),
        P("expert", None, None),
        P("expert", None, "tensor"),
    )
    return jax.shard_map(local, mesh=mesh, in_specs=in_specs, out_specs=out_specs, check_vma=False)
```

```python
import functools

import jax
import jax.numpy as jnp
from jax import lax
from jax.experimental import pallas as pl
from jax.experimental.pallas import tpu as pltpu
from jax.sharding import PartitionSpec as P

adapter_scale = 2.0
f32 = jnp.float32
bf16 = jnp.bfloat16
highest = lax.Precision.HIGHEST
vmem_limit = 52 * 1024 * 1024
lanes = 128


def send(value, axis, step):
    return lax.ppermute(value, axis, [(i, i ^ step) for i in range(lax.axis_size(axis))])


def gather(value, axis):
    return [value] + [send(value, axis, step) for step in range(1, lax.axis_size(axis))]


def swap(values, axis, steps=None):
    steps = range(len(values)) if steps is None else steps
    return [send(value, axis, step) if step else value for value, step in zip(values, steps)]


def after(value, *others):
    return lax.optimization_barrier((value, *others))[0]


def total(values):
    result = values[0].astype(f32)
    for value in values[1:]:
        result = result + value.astype(f32)
    return result


def dot(left, right, left_dim, right_dim, **options):
    return lax.dot_general(
        left, right, (((left_dim,), (right_dim,)), ((), ())), preferred_element_type=f32, **options
    )


def row_copies(place, own, other, scratch, sems, step, per_block):
    rows, width = scratch.shape[1], own[0].shape[1]
    slot = lax.rem(step, 2)
    first = pl.multiple_of(lax.rem(step, per_block) * rows, rows)

    def both(block):
        return [
            pltpu.make_async_copy(
                ref.at[pl.ds(first, rows)],
                scratch.at[slot, :, pl.ds(pl.multiple_of(side * width, width), width)],
                sems.at[slot, half],
            )
            for half, (ref, side) in enumerate(((own[block], place[1]), (other[block], 1 - place[1])))
        ]

    return [both(block) for block in range(len(own))]


def start_rows(place, own, other, scratch, sems, step, per_block):
    for block, copies in enumerate(row_copies(place, own, other, scratch, sems, step, per_block)):
        pl.when(step // per_block == block)(functools.partial(start, copies))


def wait_rows(place, own, other, scratch, sems, step, per_block):
    wait(row_copies(place, own, other, scratch, sems, step, per_block)[0])


def start(copies):
    for copy in copies:
        copy.start()


def wait(copies):
    for copy in copies:
        copy.wait()


def low_kernel(experts, per_block, place, *refs):
    own, other, refs = refs[:experts], refs[experts : 2 * experts], refs[2 * experts :]
    adapter_in, out, x_scratch, x_sems = refs
    step, steps = pl.program_id(0), pl.num_programs(0)
    pl.when(step == 0)(lambda: start_rows(place, own, other, x_scratch, x_sems, step, per_block))
    pl.when(step + 1 < steps)(lambda: start_rows(place, own, other, x_scratch, x_sems, step + 1, per_block))
    wait_rows(place, own, other, x_scratch, x_sems, step, per_block)
    out[...] = dot(x_scratch[lax.rem(step, 2)], adapter_in[...], 1, 1).astype(bf16)


def low(place, own, other, adapter_in, rows):
    experts = len(own)
    block_rows, share = own[0].shape
    rank = adapter_in.shape[0]
    return pl.pallas_call(
        functools.partial(low_kernel, experts, block_rows // rows),
        out_shape=jax.ShapeDtypeStruct((experts * block_rows, rank), bf16),
        grid_spec=pltpu.PrefetchScalarGridSpec(
            num_scalar_prefetch=1,
            grid=(experts * block_rows // rows,),
            in_specs=[pl.BlockSpec(memory_space=pl.ANY)] * (2 * experts)
            + [pl.BlockSpec(adapter_in.shape, lambda i, place: (0, 0))],
            out_specs=pl.BlockSpec((rows, rank), lambda i, place: (i, 0)),
            scratch_shapes=[pltpu.VMEM((2, rows, 2 * share), bf16), pltpu.SemaphoreType.DMA((2, 2))],
        ),
        compiler_params=pltpu.CompilerParams(vmem_limit_bytes=vmem_limit),
        name="low_rank",
    )(place, *own, *other, adapter_in)


def forward_kernel(experts, per_block, capacity, place, *refs):
    own, other, refs = refs[:experts], refs[experts : 2 * experts], refs[2 * experts :]
    low_rank, adapter_part, parts, refs = refs[0], refs[1], refs[2], refs[3:]
    groups = parts.shape[0]
    hidden, activated, slot_logits, tag_down = refs[:4]
    weight, tag_parts, x_scratch, added, weight_sems, tag_sems, x_sems = refs[4:]
    step, steps = pl.program_id(0), pl.num_programs(0)
    chunks, depth, pair = weight.shape[0], weight.shape[1] // groups, weight.shape[2]
    width, half = pair // 2, tag_parts.shape[2]
    copy = pltpu.make_async_copy

    def weight_copies(chunk):
        for k in range(groups):
            source = parts.at[k, chunk, pl.ds(0, depth)]
            yield copy(source, weight.at[chunk, pl.ds(k * depth, depth)], weight_sems.at[k, chunk])

    def tag_copies():
        for k in range(groups):
            yield copy(parts.at[k, :, pl.ds(depth, half)], tag_parts.at[k], tag_sems.at[k])

    @pl.when(step == 0)
    def _():
        start_rows(place, own, other, x_scratch, x_sems, step, per_block)
        for chunk in range(chunks):
            start(weight_copies(chunk))
        start(tag_copies())

    @pl.when(step + 1 < steps)
    def _():
        start_rows(place, own, other, x_scratch, x_sems, step + 1, per_block)

    @pl.when(step == 0)
    def _():
        for chunk in range(chunks):
            wait(weight_copies(chunk))
        wait(tag_copies())
        summed = jnp.sum(tag_parts[...].astype(f32), axis=0).astype(bf16)
        for chunk in range(chunks):
            columns = slice(chunk * width, (chunk + 1) * width)
            tag_down[:half, columns] = summed[chunk, :, :width]
            tag_down[half:, columns] = summed[chunk, :, width:]

    added[...] = adapter_scale * dot(low_rank[...], adapter_part[...], 1, 0)
    wait_rows(place, own, other, x_scratch, x_sems, step, per_block)
    slot = lax.rem(step, 2)
    for chunk in range(chunks):
        columns = slice(chunk * width, (chunk + 1) * width)
        both = dot(x_scratch[slot], weight[chunk], 1, 0)
        gate_acc = both[:, :width]
        act = gate_acc / (1.0 + jnp.exp(-gate_acc))
        activated[:, columns] = act.astype(bf16)
        hidden[:, columns] = (act * (both[:, width:] + added[:, columns])).astype(bf16)
    slot_logits[...] = jnp.zeros_like(slot_logits)
    logits = dot(tag_down[...], hidden[...], 1, 1).astype(bf16)
    for piece in range(logits.shape[1] // capacity):
        slot_logits[:, piece * lanes : piece * lanes + capacity] = logits[
            :, piece * capacity : (piece + 1) * capacity
        ]


def forward(place, own, other, parts, low_rank, adapter_part, tags, rows, capacity):
    groups, chunks, part_rows, pair = parts.shape
    width, depth = chunks * pair // 2, part_rows - tags // 2
    experts = len(own)
    block_rows, share = own[0].shape
    slots = experts * block_rows
    rank = low_rank.shape[1]
    wide = rows // capacity * lanes
    whole = lambda array: pl.BlockSpec(array.shape, lambda i, place: (0, 0))
    anywhere = pl.BlockSpec(memory_space=pl.ANY)
    return pl.pallas_call(
        functools.partial(forward_kernel, experts, block_rows // rows, capacity),
        out_shape=(
            jax.ShapeDtypeStruct((slots, width), bf16),
            jax.ShapeDtypeStruct((slots, width), bf16),
            jax.ShapeDtypeStruct((tags, slots // capacity * lanes), bf16),
            jax.ShapeDtypeStruct((tags, width), bf16),
        ),
        grid_spec=pltpu.PrefetchScalarGridSpec(
            num_scalar_prefetch=1,
            grid=(slots // rows,),
            in_specs=[anywhere] * (2 * experts)
            + [pl.BlockSpec((rows, rank), lambda i, place: (i, 0)), whole(adapter_part), anywhere],
            out_specs=(
                pl.BlockSpec((rows, width), lambda i, place: (i, 0)),
                pl.BlockSpec((rows, width), lambda i, place: (i, 0)),
                pl.BlockSpec((tags, wide), lambda i, place: (0, i)),
                pl.BlockSpec((tags, width), lambda i, place: (0, 0)),
            ),
            scratch_shapes=[
                pltpu.VMEM((chunks, groups * depth, pair), bf16),
                pltpu.VMEM((groups, chunks, tags // 2, pair), bf16),
                pltpu.VMEM((2, rows, 2 * share), bf16),
                pltpu.VMEM((rows, width), f32),
                pltpu.SemaphoreType.DMA((groups, chunks)),
                pltpu.SemaphoreType.DMA((groups,)),
                pltpu.SemaphoreType.DMA((2, 2)),
            ],
        ),
        compiler_params=pltpu.CompilerParams(vmem_limit_bytes=vmem_limit),
        name="gate_up",
    )(place, *own, *other, low_rank, adapter_part, parts)


def tag_kernel(pieces, *refs):
    parts, (token_logits, combine, labels, slot_grad) = refs[:pieces], refs[pieces:]
    slot_logits = total([part[...] for part in parts])
    logits = token_logits[...] + dot(slot_logits, combine[...], 1, 0, precision=highest)
    exp_logits = jnp.exp(logits)
    probability = exp_logits / jnp.sum(exp_logits, axis=0, keepdims=True)
    hot = labels[...] == lax.broadcasted_iota(jnp.int32, logits.shape, 0)
    logit_grad = probability - jnp.where(hot, f32(1.0), f32(0.0))
    slot_grad[...] = dot(logit_grad, combine[...], 1, 1, precision=highest).astype(bf16)


def column_chunks(count):
    size = min(count, 2 * lanes)
    return [slice(at, at + size) for at in range(0, count, size)]


def down_kernel(first, near_count, capacity, place, hidden, *refs):
    weight, sems = refs[-2:]
    count = sems.shape[0]
    downs, nears, outs = refs[:count], refs[count : count + near_count], refs[count + near_count : -2]
    step, steps = pl.program_id(0), pl.num_programs(0)
    width = downs[0].shape[1]

    @pl.when(step == 0)
    def _():
        copies = []
        for k, down in enumerate(downs):
            column = pl.multiple_of(lax.rem(place[0] ^ (first + k), count) * width, width)
            copies.append(pltpu.make_async_copy(down, weight.at[:, pl.ds(column, width)], sems.at[k]))
        start(copies)
        wait(copies)

    per_step = hidden.shape[0] // capacity
    per_block = 2 * count // per_step

    def multiply(ref):
        for columns in column_chunks(ref.shape[3]):
            value = dot(hidden[...], weight[:, columns], 1, 0).astype(bf16)
            for piece in range(per_step):
                k = lax.rem(step, per_block) * per_step + piece
                ref[place[0] ^ k, 0, :, columns] = value[piece * capacity : (piece + 1) * capacity]

    def far(near, send, keep):
        multiply(send)
        keep[...] = near[...]

    def both(near, send, keep):
        pl.when(place[2] == 0)(lambda: far(near, send, keep))
        pl.when(place[2] == 1)(lambda: far(near, keep, send))

    chunks = near_count or len(outs)
    for chunk in range(chunks):
        if near_count:
            work = functools.partial(both, nears[chunk], outs[chunk], outs[chunks + chunk])
        else:
            work = functools.partial(multiply, outs[chunk])
        pl.when(step // (steps // chunks) == chunk)(work)


def chunk_block(first, count, per_block, step, place):
    return 0, jnp.clip(step - first, 0, count - 1) // per_block, 0, 0


def down(place, hidden, rows, downs, first, nears, chunks, capacity, name):
    slots, (width, part) = hidden.shape[0], downs[0].shape
    share = part * len(downs)
    half = slots // chunks // rows
    results = 2 * chunks if nears else chunks
    groups = 2 * len(downs)
    per_block = groups * capacity // rows
    specs = [
        pl.BlockSpec((groups, 1, capacity, share), functools.partial(chunk_block, chunk * half, half, per_block))
        for chunk in range(chunks)
    ]
    return pl.pallas_call(
        functools.partial(down_kernel, first, len(nears), capacity),
        out_shape=[jax.ShapeDtypeStruct((groups, half // per_block, capacity, share), bf16)] * results,
        grid_spec=pltpu.PrefetchScalarGridSpec(
            num_scalar_prefetch=1,
            grid=(slots // rows,),
            in_specs=[
                pl.BlockSpec((rows, width), lambda i, place: ((chunks - 1 - i // half) * half + lax.rem(i, half), 0))
            ]
            + [pl.BlockSpec(memory_space=pl.ANY)] * len(downs)
            + (specs if nears else []),
            out_specs=specs * (results // chunks),
            scratch_shapes=[pltpu.VMEM((width, share), bf16), pltpu.SemaphoreType.DMA((len(downs),))],
        ),
        compiler_params=pltpu.CompilerParams(vmem_limit_bytes=62 * 1024 * 1024),
        name=name,
    )(place, hidden, *downs, *nears)


def pack_kernel(place, gate, up, down, tag_part, out):
    depth, width = gate.shape
    product = dot(tag_part[...], down[...], 0, 1).astype(bf16)
    half = product.shape[0] // 2
    for chunk in range(width // lanes):
        columns = slice(chunk * lanes, (chunk + 1) * lanes)
        out[0, chunk, :depth, :lanes] = gate[:, columns]
        out[0, chunk, :depth, lanes:] = up[:, columns]
        out[0, chunk, depth:, :lanes] = product[:half, columns]
        out[0, chunk, depth:, lanes:] = product[half:, columns]


def pack(place, gate, up, down, tag_weight, groups):
    depth, width = gate.shape
    part, tags = width // groups, tag_weight.shape[1]
    if part % lanes:
        tag_part = lax.dynamic_slice_in_dim(tag_weight, place[0] * depth, depth, 0)
        product = dot(tag_part, down, 0, 1).astype(bf16)
        rows = [jnp.concatenate([gate, product[: tags // 2]]), jnp.concatenate([up, product[tags // 2 :]])]
        rows = jnp.stack(rows).reshape(2, depth + tags // 2, groups, part)
        return rows.transpose(2, 1, 0, 3).reshape(groups, 1, depth + tags // 2, 2 * part)
    return pl.pallas_call(
        pack_kernel,
        out_shape=jax.ShapeDtypeStruct((groups, part // lanes, depth + tags // 2, 2 * lanes), bf16),
        grid_spec=pltpu.PrefetchScalarGridSpec(
            num_scalar_prefetch=1,
            grid=(groups,),
            in_specs=[
                pl.BlockSpec((depth, part), lambda i, place: (0, i)),
                pl.BlockSpec((depth, part), lambda i, place: (0, i)),
                pl.BlockSpec((part, depth), lambda i, place: (i, 0)),
                pl.BlockSpec((depth, tags), lambda i, place: (place[0], 0)),
            ],
            out_specs=pl.BlockSpec((1, part // lanes, depth + tags // 2, 2 * lanes), lambda i, place: (i, 0, 0, 0)),
        ),
        compiler_params=pltpu.CompilerParams(vmem_limit_bytes=vmem_limit),
        name="pack",
    )(place, gate, up, down, tag_weight)


def backward_kernel(experts, per_block, capacity, place, *refs):
    own, other, refs = refs[:experts], refs[experts : 2 * experts], refs[2 * experts :]
    *slot_grad, tag_down, activated, low_rank, adapter_part, out_grad, in_grad, grads, x_scratch, x_sems = refs
    step, steps = pl.program_id(0), pl.num_programs(0)

    @pl.when(step == 0)
    def _():
        start_rows(place, own, other, x_scratch, x_sems, step, per_block)
        out_grad[...] = jnp.zeros_like(out_grad)
        in_grad[...] = jnp.zeros_like(in_grad)

    @pl.when(step + 1 < steps)
    def _():
        start_rows(place, own, other, x_scratch, x_sems, step + 1, per_block)

    pieces = activated.shape[0] // capacity
    for part in range(per_block):

        @pl.when(lax.rem(step, per_block) == part)
        def _():
            for piece in range(pieces):
                grads[piece] = slot_grad[part * pieces + piece][...]

    hidden_grad = jnp.concatenate([dot(grads[piece][:, :capacity], tag_down[...], 0, 0) for piece in range(pieces)])
    up_grad = (hidden_grad * activated[...].astype(f32)).astype(bf16)
    out_grad[...] += adapter_scale * dot(low_rank[...], up_grad, 0, 0)
    low_grad = (adapter_scale * dot(adapter_part[...], up_grad, 1, 1)).astype(bf16)
    wait_rows(place, own, other, x_scratch, x_sems, step, per_block)
    in_grad[...] += dot(low_grad, x_scratch[lax.rem(step, 2)], 1, 0)


def backward(place, own, other, slot_grad, tag_down, activated, low_rank, adapter_part, rows, capacity):
    experts = len(own)
    block_rows, share = own[0].shape
    per_block = block_rows // rows
    tags, width = tag_down.shape
    slots, rank = low_rank.shape
    whole = lambda shape: pl.BlockSpec(shape, lambda i, place: (0, 0))
    anywhere = pl.BlockSpec(memory_space=pl.ANY)
    return pl.pallas_call(
        functools.partial(backward_kernel, experts, per_block, capacity),
        out_shape=(
            jax.ShapeDtypeStruct((rank, width), f32),
            jax.ShapeDtypeStruct((rank, 2 * share), f32),
        ),
        grid_spec=pltpu.PrefetchScalarGridSpec(
            num_scalar_prefetch=1,
            grid=(slots // rows,),
            in_specs=[anywhere] * (2 * experts)
            + [
                *[pl.BlockSpec((tags, lanes), lambda i, place: (0, i // per_block))] * len(slot_grad),
                whole(tag_down.shape),
                pl.BlockSpec((rows, width), lambda i, place: (i, 0)),
                pl.BlockSpec((rows, rank), lambda i, place: (i, 0)),
                whole(adapter_part.shape),
            ],
            out_specs=(whole((rank, width)), whole((rank, 2 * share))),
            scratch_shapes=[
                pltpu.VMEM((rows // capacity, tags, lanes), bf16),
                pltpu.VMEM((2, rows, 2 * share), bf16),
                pltpu.SemaphoreType.DMA((2, 2)),
            ],
        ),
        compiler_params=pltpu.CompilerParams(vmem_limit_bytes=vmem_limit),
        name="adapter_grad",
    )(place, *own, *other, *slot_grad, tag_down, activated, low_rank, adapter_part)


def finish_kernel(place, *refs):
    both, (in_total, out_total) = refs[:-2], refs[-2:]
    width = in_total.shape[1]
    in_total[...] = total([ref[:, :width] for ref in both])
    part = both[0].shape[1] - width
    for k, ref in enumerate(both):
        column = pl.multiple_of((place[0] ^ k) * part, part)
        out_total[:, pl.ds(column, part)] = ref[:, width:].astype(f32)


def finish(place, both, width):
    rank, part, groups = both[0].shape[0], both[0].shape[1] - width, len(both)
    if part % lanes:
        out_total = jnp.zeros((rank, groups * part), f32)
        for k, value in enumerate(both):
            value = value[:, width:].astype(f32)
            out_total = lax.dynamic_update_slice_in_dim(out_total, value, (place[0] ^ k) * part, 1)
        return total([value[:, :width] for value in both]), out_total
    whole = lambda shape: pl.BlockSpec(shape, lambda i, place: (0, 0))
    shapes = (rank, width), (rank, groups * part)
    return pl.pallas_call(
        finish_kernel,
        out_shape=[jax.ShapeDtypeStruct(shape, f32) for shape in shapes],
        grid_spec=pltpu.PrefetchScalarGridSpec(
            num_scalar_prefetch=1,
            grid=(1,),
            in_specs=[whole(value.shape) for value in both],
            out_specs=[whole(shape) for shape in shapes],
        ),
        compiler_params=pltpu.CompilerParams(vmem_limit_bytes=vmem_limit),
        name="finish",
    )(place, *both)


def local(
    tokens,
    expert_ids,
    gate_values,
    tag_labels,
    w_gate,
    w_up,
    w_down,
    adapter_in,
    adapter_out,
    tag_weight,
):
    experts = lax.axis_size("expert")
    groups = lax.axis_size("dp")
    dp, expert, tensor = lax.axis_index("dp"), lax.axis_index("expert"), lax.axis_index("tensor")
    upper = dp // (groups // 2)
    place = jnp.stack([dp, tensor, upper ^ tensor]).astype(jnp.int32)
    tok_count, model_width = tokens.shape
    share_width = model_width // lax.axis_size("tensor")
    capacity = 3 * tok_count // experts
    feature_part = w_gate.shape[1]
    hidden_part = w_gate.shape[2] // groups
    tags = tag_weight.shape[1]
    rank = adapter_in.shape[1]
    block_rows = groups * capacity
    rows = 4 * capacity

    member = expert_ids[None, :, :] == jnp.arange(experts, dtype=jnp.int32)[:, None, None]
    used = jnp.any(member, axis=2).astype(f32)
    weight = jnp.sum(jnp.where(member, gate_values[None], f32(0.0)), axis=2)
    upto = (jnp.arange(tok_count)[:, None] <= jnp.arange(tok_count)[None, :]).astype(f32)
    code = used * dot(used, upto, 1, 0)
    steps = sorted(range(experts), key=lambda step: (step % 2, step))
    order = jnp.array(steps, jnp.int32) ^ expert
    places = jnp.arange(1, lanes + 1, dtype=jnp.int32).astype(f32)
    own_match = code[order][:, None, :] == places[None, :, None]
    combine = jnp.where(own_match, weight[order][:, None, :], f32(0.0)).reshape(experts * lanes, tok_count)

    token_half = lax.dynamic_slice_in_dim(tokens, tensor * share_width, share_width, 1)
    code_rows = jnp.pad(code.astype(bf16), ((0, 8 - experts), (0, share_width - tok_count)))
    plane = gather(jnp.concatenate([token_half, code_rows], axis=0), "dp")
    parts = pack(place, w_gate[0], w_up[0], w_down[0], tag_weight, groups)
    plane_parts = plane
    plane = jnp.stack(plane)
    plane_code = plane[:, tok_count : tok_count + experts, :tok_count].astype(f32)
    plane_tokens = plane[:, :tok_count]
    downs = [lax.dynamic_slice_in_dim(w_down[0], (dp ^ k) * hidden_part, hidden_part, 0) for k in range(groups)]
    plane_tokens = after(plane_tokens, parts, *downs)
    parts = lax.all_to_all(after(parts, *plane_parts), "dp", split_axis=0, concat_axis=0, tiled=True)
    x_own = []
    for j in steps:
        target_code = lax.dynamic_index_in_dim(plane_code, expert ^ j, 1, keepdims=False)
        match = (target_code[:, None, :] == places[None, :capacity, None]).astype(bf16)
        outgoing = jnp.einsum("gst,gtd->gsd", match, plane_tokens, preferred_element_type=f32).astype(bf16)
        x_own.append(outgoing.reshape(block_rows, share_width))
    x_own = swap(x_own, "expert", steps)
    x_other = [send(value, "tensor", 1) for value in x_own]
    low_rank = low(place, x_own, x_other, adapter_in[0], rows)
    token_logits = dot(tag_weight, tokens, 0, 1)
    parts = after(parts, low_rank, combine, token_logits)
    downs = swap([after(piece, parts) for piece in downs], "dp")
    adapter_part = lax.dynamic_slice_in_dim(adapter_out[0], dp * hidden_part, hidden_part, 1)

    hidden, activated, slot_logits, tag_down = forward(
        place, x_own, x_other, parts, low_rank, adapter_part, tags, rows, capacity
    )

    slot_logits = (slot_logits.astype(f32) + send(slot_logits, "tensor", 1).astype(f32)).astype(bf16)
    plane_lanes = groups * lanes
    pieces = [slot_logits[:, j * plane_lanes : (j + 1) * plane_lanes] for j in range(experts)]
    pieces = swap(pieces, "expert", steps)

    chunks = [(experts // 2, experts // 2), (0, experts // 2)]
    half = groups // 2

    def change(part):
        return lax.all_to_all(part, "dp", split_axis=0, concat_axis=0, tiled=True)

    near = down(place, hidden, rows, downs[:half], 0, [], len(chunks), capacity, "down_near")
    hidden = after(hidden, near[0], *pieces)
    pieces = [
        jnp.concatenate([piece[:, k * lanes : (k + 1) * lanes] for piece in pieces], axis=1) for k in range(groups)
    ]
    pieces = swap(pieces, "dp")
    halves = down(place, hidden, rows, downs[half:], half, near, len(chunks), capacity, "down_far")
    others, kept = [send(value, "tensor", 1) for value in halves[: len(chunks)]], halves[len(chunks) :]

    def own(chunk, came):
        value = (kept[chunk].astype(f32) + came.astype(f32)).astype(bf16)
        return value.reshape(groups, -1, share_width)

    first = own(0, after(others[0], *pieces))

    pieces[0] = after(pieces[0], first)
    slot_grad = pl.pallas_call(
        functools.partial(tag_kernel, groups),
        out_shape=jax.ShapeDtypeStruct((tags, experts * lanes), bf16),
        compiler_params=pltpu.CompilerParams(vmem_limit_bytes=vmem_limit),
        name="tag_grad",
    )(*pieces, token_logits, combine, tag_labels[None, :])
    slot_grad = swap([slot_grad[:, j * lanes : (j + 1) * lanes] for j in range(experts)], "expert", steps)
    second = own(1, after(others[1], *slot_grad))
    slot_grad[0] = after(slot_grad[0], second)
    slot_grad = gather(jnp.concatenate(slot_grad, axis=1), "dp")
    came = [change(first), change(after(second, *slot_grad[1:]))]

    sums = [jnp.sum(came[0].astype(f32), axis=0).astype(bf16)]
    slot_grad[0] = after(slot_grad[0], sums[0])
    out_local, in_local = backward(
        place, x_own, x_other, slot_grad, tag_down, activated, low_rank, adapter_part, rows, capacity
    )
    returned = [None] * experts

    def give_back(chunk):
        first, count = chunks[chunk]
        for j in range(first, first + count):
            kept = sums[chunk][(j - first) * capacity : (j - first + 1) * capacity]
            returned[j] = send(kept, "expert", steps[j]) if steps[j] else kept

    give_back(0)
    in_local = after(in_local, *returned[chunks[0][0] :])
    in_local = in_local + send(in_local.astype(bf16), "tensor", 1).astype(f32)
    both = gather(jnp.concatenate([in_local, out_local], axis=1).astype(bf16), "dp")
    sums.append(jnp.sum(came[1].astype(f32), axis=0).astype(bf16))
    give_back(1)
    both[0] = after(both[0], sums[-1])
    in_total, out_total = finish(place, both, model_width)
    layer_out = token_half.astype(f32)
    for j in range(experts):
        kept = combine[j * lanes : j * lanes + capacity]
        layer_out = layer_out + dot(kept, returned[j].astype(f32), 0, 0, precision=highest)
    layer_out = layer_out.astype(bf16)
    return (layer_out, in_total[None], out_total[None])


def solution(mesh):
    in_specs = (
        P(("dp", "expert"), None),
        P(("dp", "expert"), None),
        P(("dp", "expert"), None),
        P(("dp", "expert")),
        P("expert", "dp", "tensor"),
        P("expert", "dp", "tensor"),
        P("expert", "tensor", "dp"),
        P("expert", None, None),
        P("expert", None, "tensor"),
        P(),
    )
    out_specs = (
        P(("dp", "expert"), "tensor"),
        P("expert", None, None),
        P("expert", None, "tensor"),
    )
    return jax.shard_map(local, mesh=mesh, in_specs=in_specs, out_specs=out_specs, check_vma=False)
```

```python
import functools

import jax
import jax.numpy as jnp
from jax import lax
from jax.experimental import pallas as pl
from jax.experimental.pallas import tpu as pltpu
from jax.sharding import PartitionSpec as P

adapter_scale = 2.0
f32 = jnp.float32
bf16 = jnp.bfloat16
highest = lax.Precision.HIGHEST
vmem_limit = 52 * 1024 * 1024
lanes = 128


def send(value, axis, step):
    return lax.ppermute(value, axis, [(i, i ^ step) for i in range(lax.axis_size(axis))])


def gather(value, axis):
    return [value] + [send(value, axis, step) for step in range(1, lax.axis_size(axis))]


def swap(values, axis, steps=None):
    steps = range(len(values)) if steps is None else steps
    return [send(value, axis, step) if step else value for value, step in zip(values, steps)]


def after(value, *others):
    return lax.optimization_barrier((value, *others))[0]


def total(values):
    result = values[0].astype(f32)
    for value in values[1:]:
        result = result + value.astype(f32)
    return result


def dot(left, right, left_dim, right_dim, **options):
    return lax.dot_general(
        left, right, (((left_dim,), (right_dim,)), ((), ())), preferred_element_type=f32, **options
    )


def row_copies(place, own, other, scratch, sems, step, per_block):
    rows, width = scratch.shape[1], own[0].shape[1]
    slot = lax.rem(step, 2)
    first = pl.multiple_of(lax.rem(step, per_block) * rows, rows)

    def both(block):
        return [
            pltpu.make_async_copy(
                ref.at[pl.ds(first, rows)],
                scratch.at[slot, :, pl.ds(pl.multiple_of(side * width, width), width)],
                sems.at[slot, half],
            )
            for half, (ref, side) in enumerate(((own[block], place[1]), (other[block], 1 - place[1])))
        ]

    return [both(block) for block in range(len(own))]


def start_rows(place, own, other, scratch, sems, step, per_block):
    for block, copies in enumerate(row_copies(place, own, other, scratch, sems, step, per_block)):
        pl.when(step // per_block == block)(functools.partial(start, copies))


def wait_rows(place, own, other, scratch, sems, step, per_block):
    wait(row_copies(place, own, other, scratch, sems, step, per_block)[0])


def start(copies):
    for copy in copies:
        copy.start()


def wait(copies):
    for copy in copies:
        copy.wait()


def low_kernel(experts, per_block, place, *refs):
    own, other, refs = refs[:experts], refs[experts : 2 * experts], refs[2 * experts :]
    adapter_in, out, x_scratch, x_sems = refs
    step, steps = pl.program_id(0), pl.num_programs(0)
    pl.when(step == 0)(lambda: start_rows(place, own, other, x_scratch, x_sems, step, per_block))
    pl.when(step + 1 < steps)(lambda: start_rows(place, own, other, x_scratch, x_sems, step + 1, per_block))
    wait_rows(place, own, other, x_scratch, x_sems, step, per_block)
    out[...] = dot(x_scratch[lax.rem(step, 2)], adapter_in[...], 1, 1).astype(bf16)


def low(place, own, other, adapter_in, rows):
    experts = len(own)
    block_rows, share = own[0].shape
    rank = adapter_in.shape[0]
    return pl.pallas_call(
        functools.partial(low_kernel, experts, block_rows // rows),
        out_shape=jax.ShapeDtypeStruct((experts * block_rows, rank), bf16),
        grid_spec=pltpu.PrefetchScalarGridSpec(
            num_scalar_prefetch=1,
            grid=(experts * block_rows // rows,),
            in_specs=[pl.BlockSpec(memory_space=pl.ANY)] * (2 * experts)
            + [pl.BlockSpec(adapter_in.shape, lambda i, place: (0, 0))],
            out_specs=pl.BlockSpec((rows, rank), lambda i, place: (i, 0)),
            scratch_shapes=[pltpu.VMEM((2, rows, 2 * share), bf16), pltpu.SemaphoreType.DMA((2, 2))],
        ),
        compiler_params=pltpu.CompilerParams(vmem_limit_bytes=vmem_limit),
        name="low_rank",
    )(place, *own, *other, adapter_in)


def forward_kernel(experts, per_block, capacity, place, *refs):
    own, other, refs = refs[:experts], refs[experts : 2 * experts], refs[2 * experts :]
    low_rank, adapter_part, parts, refs = refs[0], refs[1], refs[2], refs[3:]
    groups = parts.shape[0]
    hidden, activated, slot_logits, tag_down = refs[:4]
    weight, tag_parts, x_scratch, added, weight_sems, tag_sems, x_sems = refs[4:]
    step, steps = pl.program_id(0), pl.num_programs(0)
    chunks, depth, pair = weight.shape[0], weight.shape[1] // groups, weight.shape[2]
    width, half = pair // 2, tag_parts.shape[2]
    copy = pltpu.make_async_copy

    def weight_copies(chunk):
        for k in range(groups):
            source = parts.at[k, chunk, pl.ds(0, depth)]
            yield copy(source, weight.at[chunk, pl.ds(k * depth, depth)], weight_sems.at[k, chunk])

    def tag_copies():
        for k in range(groups):
            yield copy(parts.at[k, :, pl.ds(depth, half)], tag_parts.at[k], tag_sems.at[k])

    @pl.when(step == 0)
    def _():
        start_rows(place, own, other, x_scratch, x_sems, step, per_block)
        for chunk in range(chunks):
            start(weight_copies(chunk))
        start(tag_copies())

    @pl.when(step + 1 < steps)
    def _():
        start_rows(place, own, other, x_scratch, x_sems, step + 1, per_block)

    @pl.when(step == 0)
    def _():
        for chunk in range(chunks):
            wait(weight_copies(chunk))
        wait(tag_copies())
        summed = jnp.sum(tag_parts[...].astype(f32), axis=0).astype(bf16)
        for chunk in range(chunks):
            columns = slice(chunk * width, (chunk + 1) * width)
            tag_down[:half, columns] = summed[chunk, :, :width]
            tag_down[half:, columns] = summed[chunk, :, width:]

    added[...] = adapter_scale * dot(low_rank[...], adapter_part[...], 1, 0)
    wait_rows(place, own, other, x_scratch, x_sems, step, per_block)
    slot = lax.rem(step, 2)
    for chunk in range(chunks):
        columns = slice(chunk * width, (chunk + 1) * width)
        both = dot(x_scratch[slot], weight[chunk], 1, 0)
        gate_acc = both[:, :width]
        act = gate_acc / (1.0 + jnp.exp(-gate_acc))
        activated[:, columns] = act.astype(bf16)
        hidden[:, columns] = (act * (both[:, width:] + added[:, columns])).astype(bf16)
    slot_logits[...] = jnp.zeros_like(slot_logits)
    logits = dot(tag_down[...], hidden[...], 1, 1).astype(bf16)
    for piece in range(logits.shape[1] // capacity):
        slot_logits[:, piece * lanes : piece * lanes + capacity] = logits[
            :, piece * capacity : (piece + 1) * capacity
        ]


def forward(place, own, other, parts, low_rank, adapter_part, tags, rows, capacity):
    groups, chunks, part_rows, pair = parts.shape
    width, depth = chunks * pair // 2, part_rows - tags // 2
    experts = len(own)
    block_rows, share = own[0].shape
    slots = experts * block_rows
    rank = low_rank.shape[1]
    wide = rows // capacity * lanes
    whole = lambda array: pl.BlockSpec(array.shape, lambda i, place: (0, 0))
    anywhere = pl.BlockSpec(memory_space=pl.ANY)
    return pl.pallas_call(
        functools.partial(forward_kernel, experts, block_rows // rows, capacity),
        out_shape=(
            jax.ShapeDtypeStruct((slots, width), bf16),
            jax.ShapeDtypeStruct((slots, width), bf16),
            jax.ShapeDtypeStruct((tags, slots // capacity * lanes), bf16),
            jax.ShapeDtypeStruct((tags, width), bf16),
        ),
        grid_spec=pltpu.PrefetchScalarGridSpec(
            num_scalar_prefetch=1,
            grid=(slots // rows,),
            in_specs=[anywhere] * (2 * experts)
            + [pl.BlockSpec((rows, rank), lambda i, place: (i, 0)), whole(adapter_part), anywhere],
            out_specs=(
                pl.BlockSpec((rows, width), lambda i, place: (i, 0)),
                pl.BlockSpec((rows, width), lambda i, place: (i, 0)),
                pl.BlockSpec((tags, wide), lambda i, place: (0, i)),
                pl.BlockSpec((tags, width), lambda i, place: (0, 0)),
            ),
            scratch_shapes=[
                pltpu.VMEM((chunks, groups * depth, pair), bf16),
                pltpu.VMEM((groups, chunks, tags // 2, pair), bf16),
                pltpu.VMEM((2, rows, 2 * share), bf16),
                pltpu.VMEM((rows, width), f32),
                pltpu.SemaphoreType.DMA((groups, chunks)),
                pltpu.SemaphoreType.DMA((groups,)),
                pltpu.SemaphoreType.DMA((2, 2)),
            ],
        ),
        compiler_params=pltpu.CompilerParams(vmem_limit_bytes=vmem_limit),
        name="gate_up",
    )(place, *own, *other, low_rank, adapter_part, parts)


def tag_kernel(pieces, *refs):
    parts, (token_logits, combine, labels, slot_grad) = refs[:pieces], refs[pieces:]
    slot_logits = total([part[...] for part in parts])
    logits = token_logits[...] + dot(slot_logits, combine[...], 1, 0, precision=highest)
    exp_logits = jnp.exp(logits)
    probability = exp_logits / jnp.sum(exp_logits, axis=0, keepdims=True)
    hot = labels[...] == lax.broadcasted_iota(jnp.int32, logits.shape, 0)
    logit_grad = probability - jnp.where(hot, f32(1.0), f32(0.0))
    slot_grad[...] = dot(logit_grad, combine[...], 1, 1, precision=highest).astype(bf16)


def column_chunks(count):
    size = min(count, 4 * lanes)
    return [slice(at, at + size) for at in range(0, count, size)]


def down_kernel(first, near_count, capacity, place, hidden, *refs):
    weight, sems = refs[-2:]
    count = sems.shape[0]
    downs, nears, outs = refs[:count], refs[count : count + near_count], refs[count + near_count : -2]
    step, steps = pl.program_id(0), pl.num_programs(0)
    width = downs[0].shape[1]

    @pl.when(step == 0)
    def _():
        copies = []
        for k, down in enumerate(downs):
            column = pl.multiple_of(lax.rem(place[0] ^ (first + k), count) * width, width)
            copies.append(pltpu.make_async_copy(down, weight.at[:, pl.ds(column, width)], sems.at[k]))
        start(copies)
        wait(copies)

    per_step = hidden.shape[0] // capacity
    per_block = 2 * count // per_step

    def multiply(ref):
        for columns in column_chunks(ref.shape[3]):
            value = dot(hidden[...], weight[:, columns], 1, 0).astype(bf16)
            for piece in range(per_step):
                k = lax.rem(step, per_block) * per_step + piece
                ref[place[0] ^ k, 0, :, columns] = value[piece * capacity : (piece + 1) * capacity]

    def far(near, send, keep):
        multiply(send)
        keep[...] = near[...]

    def both(near, send, keep):
        pl.when(place[2] == 0)(lambda: far(near, send, keep))
        pl.when(place[2] == 1)(lambda: far(near, keep, send))

    chunks = near_count or len(outs)
    for chunk in range(chunks):
        if near_count:
            work = functools.partial(both, nears[chunk], outs[chunk], outs[chunks + chunk])
        else:
            work = functools.partial(multiply, outs[chunk])
        pl.when(step // (steps // chunks) == chunk)(work)


def chunk_block(first, count, per_block, step, place):
    return 0, jnp.clip(step - first, 0, count - 1) // per_block, 0, 0


def down(place, hidden, rows, downs, first, nears, chunks, capacity, name):
    slots, (width, part) = hidden.shape[0], downs[0].shape
    share = part * len(downs)
    half = slots // chunks // rows
    results = 2 * chunks if nears else chunks
    groups = 2 * len(downs)
    per_block = groups * capacity // rows
    specs = [
        pl.BlockSpec((groups, 1, capacity, share), functools.partial(chunk_block, chunk * half, half, per_block))
        for chunk in range(chunks)
    ]
    return pl.pallas_call(
        functools.partial(down_kernel, first, len(nears), capacity),
        out_shape=[jax.ShapeDtypeStruct((groups, half // per_block, capacity, share), bf16)] * results,
        grid_spec=pltpu.PrefetchScalarGridSpec(
            num_scalar_prefetch=1,
            grid=(slots // rows,),
            in_specs=[
                pl.BlockSpec((rows, width), lambda i, place: ((chunks - 1 - i // half) * half + lax.rem(i, half), 0))
            ]
            + [pl.BlockSpec(memory_space=pl.ANY)] * len(downs)
            + (specs if nears else []),
            out_specs=specs * (results // chunks),
            scratch_shapes=[pltpu.VMEM((width, share), bf16), pltpu.SemaphoreType.DMA((len(downs),))],
        ),
        compiler_params=pltpu.CompilerParams(vmem_limit_bytes=62 * 1024 * 1024),
        name=name,
    )(place, hidden, *downs, *nears)


def pack_kernel(place, gate, up, down, tag_part, out):
    depth, width = gate.shape
    product = dot(tag_part[...], down[...], 0, 1).astype(bf16)
    half = product.shape[0] // 2
    for chunk in range(width // lanes):
        columns = slice(chunk * lanes, (chunk + 1) * lanes)
        out[0, chunk, :depth, :lanes] = gate[:, columns]
        out[0, chunk, :depth, lanes:] = up[:, columns]
        out[0, chunk, depth:, :lanes] = product[:half, columns]
        out[0, chunk, depth:, lanes:] = product[half:, columns]


def pack(place, gate, up, down, tag_weight, groups):
    depth, width = gate.shape
    part, tags = width // groups, tag_weight.shape[1]
    if part % lanes:
        tag_part = lax.dynamic_slice_in_dim(tag_weight, place[0] * depth, depth, 0)
        product = dot(tag_part, down, 0, 1).astype(bf16)
        rows = [jnp.concatenate([gate, product[: tags // 2]]), jnp.concatenate([up, product[tags // 2 :]])]
        rows = jnp.stack(rows).reshape(2, depth + tags // 2, groups, part)
        return rows.transpose(2, 1, 0, 3).reshape(groups, 1, depth + tags // 2, 2 * part)
    return pl.pallas_call(
        pack_kernel,
        out_shape=jax.ShapeDtypeStruct((groups, part // lanes, depth + tags // 2, 2 * lanes), bf16),
        grid_spec=pltpu.PrefetchScalarGridSpec(
            num_scalar_prefetch=1,
            grid=(groups,),
            in_specs=[
                pl.BlockSpec((depth, part), lambda i, place: (0, i)),
                pl.BlockSpec((depth, part), lambda i, place: (0, i)),
                pl.BlockSpec((part, depth), lambda i, place: (i, 0)),
                pl.BlockSpec((depth, tags), lambda i, place: (place[0], 0)),
            ],
            out_specs=pl.BlockSpec((1, part // lanes, depth + tags // 2, 2 * lanes), lambda i, place: (i, 0, 0, 0)),
        ),
        compiler_params=pltpu.CompilerParams(vmem_limit_bytes=vmem_limit),
        name="pack",
    )(place, gate, up, down, tag_weight)


def backward_kernel(experts, per_block, capacity, place, *refs):
    own, other, refs = refs[:experts], refs[experts : 2 * experts], refs[2 * experts :]
    *slot_grad, tag_down, activated, low_rank, adapter_part, out_grad, in_grad, grads, x_scratch, x_sems = refs
    step, steps = pl.program_id(0), pl.num_programs(0)

    @pl.when(step == 0)
    def _():
        start_rows(place, own, other, x_scratch, x_sems, step, per_block)
        out_grad[...] = jnp.zeros_like(out_grad)
        in_grad[...] = jnp.zeros_like(in_grad)

    @pl.when(step + 1 < steps)
    def _():
        start_rows(place, own, other, x_scratch, x_sems, step + 1, per_block)

    pieces = activated.shape[0] // capacity
    for part in range(per_block):

        @pl.when(lax.rem(step, per_block) == part)
        def _():
            for piece in range(pieces):
                grads[piece] = slot_grad[part * pieces + piece][...]

    hidden_grad = jnp.concatenate([dot(grads[piece][:, :capacity], tag_down[...], 0, 0) for piece in range(pieces)])
    up_grad = (hidden_grad * activated[...].astype(f32)).astype(bf16)
    out_grad[...] += adapter_scale * dot(low_rank[...], up_grad, 0, 0)
    low_grad = (adapter_scale * dot(adapter_part[...], up_grad, 1, 1)).astype(bf16)
    wait_rows(place, own, other, x_scratch, x_sems, step, per_block)
    in_grad[...] += dot(low_grad, x_scratch[lax.rem(step, 2)], 1, 0)


def backward(place, own, other, slot_grad, tag_down, activated, low_rank, adapter_part, rows, capacity):
    experts = len(own)
    block_rows, share = own[0].shape
    per_block = block_rows // rows
    tags, width = tag_down.shape
    slots, rank = low_rank.shape
    whole = lambda shape: pl.BlockSpec(shape, lambda i, place: (0, 0))
    anywhere = pl.BlockSpec(memory_space=pl.ANY)
    return pl.pallas_call(
        functools.partial(backward_kernel, experts, per_block, capacity),
        out_shape=(
            jax.ShapeDtypeStruct((rank, width), f32),
            jax.ShapeDtypeStruct((rank, 2 * share), f32),
        ),
        grid_spec=pltpu.PrefetchScalarGridSpec(
            num_scalar_prefetch=1,
            grid=(slots // rows,),
            in_specs=[anywhere] * (2 * experts)
            + [
                *[pl.BlockSpec((tags, lanes), lambda i, place: (0, i // per_block))] * len(slot_grad),
                whole(tag_down.shape),
                pl.BlockSpec((rows, width), lambda i, place: (i, 0)),
                pl.BlockSpec((rows, rank), lambda i, place: (i, 0)),
                whole(adapter_part.shape),
            ],
            out_specs=(whole((rank, width)), whole((rank, 2 * share))),
            scratch_shapes=[
                pltpu.VMEM((rows // capacity, tags, lanes), bf16),
                pltpu.VMEM((2, rows, 2 * share), bf16),
                pltpu.SemaphoreType.DMA((2, 2)),
            ],
        ),
        compiler_params=pltpu.CompilerParams(vmem_limit_bytes=vmem_limit),
        name="adapter_grad",
    )(place, *own, *other, *slot_grad, tag_down, activated, low_rank, adapter_part)


def finish_kernel(place, *refs):
    both, (in_total, out_total) = refs[:-2], refs[-2:]
    width = in_total.shape[1]
    in_total[...] = total([ref[:, :width] for ref in both])
    part = both[0].shape[1] - width
    for k, ref in enumerate(both):
        column = pl.multiple_of((place[0] ^ k) * part, part)
        out_total[:, pl.ds(column, part)] = ref[:, width:].astype(f32)


def finish(place, both, width):
    rank, part, groups = both[0].shape[0], both[0].shape[1] - width, len(both)
    if part % lanes:
        out_total = jnp.zeros((rank, groups * part), f32)
        for k, value in enumerate(both):
            value = value[:, width:].astype(f32)
            out_total = lax.dynamic_update_slice_in_dim(out_total, value, (place[0] ^ k) * part, 1)
        return total([value[:, :width] for value in both]), out_total
    whole = lambda shape: pl.BlockSpec(shape, lambda i, place: (0, 0))
    shapes = (rank, width), (rank, groups * part)
    return pl.pallas_call(
        finish_kernel,
        out_shape=[jax.ShapeDtypeStruct(shape, f32) for shape in shapes],
        grid_spec=pltpu.PrefetchScalarGridSpec(
            num_scalar_prefetch=1,
            grid=(1,),
            in_specs=[whole(value.shape) for value in both],
            out_specs=[whole(shape) for shape in shapes],
        ),
        compiler_params=pltpu.CompilerParams(vmem_limit_bytes=vmem_limit),
        name="finish",
    )(place, *both)


def local(
    tokens,
    expert_ids,
    gate_values,
    tag_labels,
    w_gate,
    w_up,
    w_down,
    adapter_in,
    adapter_out,
    tag_weight,
):
    experts = lax.axis_size("expert")
    groups = lax.axis_size("dp")
    dp, expert, tensor = lax.axis_index("dp"), lax.axis_index("expert"), lax.axis_index("tensor")
    upper = dp // (groups // 2)
    place = jnp.stack([dp, tensor, upper ^ tensor]).astype(jnp.int32)
    tok_count, model_width = tokens.shape
    share_width = model_width // lax.axis_size("tensor")
    capacity = 3 * tok_count // experts
    feature_part = w_gate.shape[1]
    hidden_part = w_gate.shape[2] // groups
    tags = tag_weight.shape[1]
    rank = adapter_in.shape[1]
    block_rows = groups * capacity
    rows = 4 * capacity

    member = expert_ids[None, :, :] == jnp.arange(experts, dtype=jnp.int32)[:, None, None]
    used = jnp.any(member, axis=2).astype(f32)
    weight = jnp.sum(jnp.where(member, gate_values[None], f32(0.0)), axis=2)
    upto = (jnp.arange(tok_count)[:, None] <= jnp.arange(tok_count)[None, :]).astype(f32)
    code = used * dot(used, upto, 1, 0)
    steps = sorted(range(experts), key=lambda step: (step % 2, step))
    order = jnp.array(steps, jnp.int32) ^ expert
    places = jnp.arange(1, lanes + 1, dtype=jnp.int32).astype(f32)
    own_match = code[order][:, None, :] == places[None, :, None]
    combine = jnp.where(own_match, weight[order][:, None, :], f32(0.0)).reshape(experts * lanes, tok_count)

    token_half = lax.dynamic_slice_in_dim(tokens, tensor * share_width, share_width, 1)
    code_rows = jnp.pad(code.astype(bf16), ((0, 8 - experts), (0, share_width - tok_count)))
    plane = gather(jnp.concatenate([token_half, code_rows], axis=0), "dp")
    parts = pack(place, w_gate[0], w_up[0], w_down[0], tag_weight, groups)
    plane_parts = plane
    plane = jnp.stack(plane)
    plane_code = plane[:, tok_count : tok_count + experts, :tok_count].astype(f32)
    plane_tokens = plane[:, :tok_count]
    downs = [lax.dynamic_slice_in_dim(w_down[0], (dp ^ k) * hidden_part, hidden_part, 0) for k in range(groups)]
    plane_tokens = after(plane_tokens, parts, *downs)
    parts = lax.all_to_all(after(parts, *plane_parts), "dp", split_axis=0, concat_axis=0, tiled=True)
    x_own = []
    for j in steps:
        target_code = lax.dynamic_index_in_dim(plane_code, expert ^ j, 1, keepdims=False)
        match = (target_code[:, None, :] == places[None, :capacity, None]).astype(bf16)
        outgoing = jnp.einsum("gst,gtd->gsd", match, plane_tokens, preferred_element_type=f32).astype(bf16)
        x_own.append(outgoing.reshape(block_rows, share_width))
    x_own = swap(x_own, "expert", steps)
    x_other = [send(value, "tensor", 1) for value in x_own]
    low_rank = low(place, x_own, x_other, adapter_in[0], rows)
    token_logits = dot(tag_weight, tokens, 0, 1)
    parts = after(parts, low_rank, combine, token_logits)
    downs = swap([after(piece, parts) for piece in downs], "dp")
    adapter_part = lax.dynamic_slice_in_dim(adapter_out[0], dp * hidden_part, hidden_part, 1)

    hidden, activated, slot_logits, tag_down = forward(
        place, x_own, x_other, parts, low_rank, adapter_part, tags, rows, capacity
    )

    slot_logits = (slot_logits.astype(f32) + send(slot_logits, "tensor", 1).astype(f32)).astype(bf16)
    plane_lanes = groups * lanes
    pieces = [slot_logits[:, j * plane_lanes : (j + 1) * plane_lanes] for j in range(experts)]
    pieces = swap(pieces, "expert", steps)

    chunks = [(experts // 2, experts // 2), (0, experts // 2)]
    half = groups // 2

    def change(part):
        return lax.all_to_all(part, "dp", split_axis=0, concat_axis=0, tiled=True)

    near = down(place, hidden, rows, downs[:half], 0, [], len(chunks), capacity, "down_near")
    hidden = after(hidden, near[0], *pieces)
    pieces = [
        jnp.concatenate([piece[:, k * lanes : (k + 1) * lanes] for piece in pieces], axis=1) for k in range(groups)
    ]
    pieces = swap(pieces, "dp")
    halves = down(place, hidden, rows, downs[half:], half, near, len(chunks), capacity, "down_far")
    others, kept = [send(value, "tensor", 1) for value in halves[: len(chunks)]], halves[len(chunks) :]

    def own(chunk, came):
        value = (kept[chunk].astype(f32) + came.astype(f32)).astype(bf16)
        return value.reshape(groups, -1, share_width)

    first = own(0, others[0])

    pieces[0] = after(pieces[0], first)
    slot_grad = pl.pallas_call(
        functools.partial(tag_kernel, groups),
        out_shape=jax.ShapeDtypeStruct((tags, experts * lanes), bf16),
        compiler_params=pltpu.CompilerParams(vmem_limit_bytes=vmem_limit),
        name="tag_grad",
    )(*pieces, token_logits, combine, tag_labels[None, :])
    slot_grad = swap([slot_grad[:, j * lanes : (j + 1) * lanes] for j in range(experts)], "expert", steps)
    second = own(1, after(others[1], *slot_grad))
    slot_grad = gather(jnp.concatenate(slot_grad, axis=1), "dp")
    came = [change(after(first, *pieces)), change(after(second, *slot_grad[1:]))]

    sums = [jnp.sum(came[0].astype(f32), axis=0).astype(bf16)]
    slot_grad[0] = after(slot_grad[0], sums[0])
    out_local, in_local = backward(
        place, x_own, x_other, slot_grad, tag_down, activated, low_rank, adapter_part, rows, capacity
    )
    returned = [None] * experts

    def give_back(chunk):
        first, count = chunks[chunk]
        for j in range(first, first + count):
            kept = sums[chunk][(j - first) * capacity : (j - first + 1) * capacity]
            returned[j] = send(kept, "expert", steps[j]) if steps[j] else kept

    give_back(0)
    in_local = after(in_local, *returned[chunks[0][0] :])
    in_local = in_local + send(in_local.astype(bf16), "tensor", 1).astype(f32)
    both = gather(jnp.concatenate([in_local, out_local], axis=1).astype(bf16), "dp")
    sums.append(jnp.sum(came[1].astype(f32), axis=0).astype(bf16))
    give_back(1)
    both[0] = after(both[0], sums[-1])
    in_total, out_total = finish(place, both, model_width)
    layer_out = token_half.astype(f32)
    for j in range(experts):
        kept = combine[j * lanes : j * lanes + capacity]
        layer_out = layer_out + dot(kept, returned[j].astype(f32), 0, 0, precision=highest)
    layer_out = layer_out.astype(bf16)
    return (layer_out, in_total[None], out_total[None])


def solution(mesh):
    in_specs = (
        P(("dp", "expert"), None),
        P(("dp", "expert"), None),
        P(("dp", "expert"), None),
        P(("dp", "expert")),
        P("expert", "dp", "tensor"),
        P("expert", "dp", "tensor"),
        P("expert", "tensor", "dp"),
        P("expert", None, None),
        P("expert", None, "tensor"),
        P(),
    )
    out_specs = (
        P(("dp", "expert"), "tensor"),
        P("expert", None, None),
        P("expert", None, "tensor"),
    )
    return jax.shard_map(local, mesh=mesh, in_specs=in_specs, out_specs=out_specs, check_vma=False)
```

```python
import functools

import jax
import jax.numpy as jnp
from jax import lax
from jax.experimental import pallas as pl
from jax.experimental.pallas import tpu as pltpu
from jax.sharding import PartitionSpec as P

adapter_scale = 2.0
f32 = jnp.float32
bf16 = jnp.bfloat16
highest = lax.Precision.HIGHEST
vmem_limit = 46 * 1024 * 1024
lanes = 128


def send(value, axis, step):
    return lax.ppermute(value, axis, [(i, i ^ step) for i in range(lax.axis_size(axis))])


def gather(value, axis):
    return [value] + [send(value, axis, step) for step in range(1, lax.axis_size(axis))]


def swap(values, axis, steps=None):
    steps = range(len(values)) if steps is None else steps
    return [send(value, axis, step) if step else value for value, step in zip(values, steps)]


def after(value, *others):
    return lax.optimization_barrier((value, *others))[0]


def total(values):
    result = values[0].astype(f32)
    for value in values[1:]:
        result = result + value.astype(f32)
    return result


def dot(left, right, left_dim, right_dim, **options):
    return lax.dot_general(
        left, right, (((left_dim,), (right_dim,)), ((), ())), preferred_element_type=f32, **options
    )


def row_copies(place, own, other, scratch, sems, step, per_block):
    rows, width = scratch.shape[1], own[0].shape[1]
    slot = lax.rem(step, 2)
    first = pl.multiple_of(lax.rem(step, per_block) * rows, rows)

    def both(block):
        return [
            pltpu.make_async_copy(
                ref.at[pl.ds(first, rows)],
                scratch.at[slot, :, pl.ds(pl.multiple_of(side * width, width), width)],
                sems.at[slot, half],
            )
            for half, (ref, side) in enumerate(((own[block], place[1]), (other[block], 1 - place[1])))
        ]

    return [both(block) for block in range(len(own))]


def start_rows(place, own, other, scratch, sems, step, per_block):
    for block, copies in enumerate(row_copies(place, own, other, scratch, sems, step, per_block)):
        pl.when(step // per_block == block)(functools.partial(start, copies))


def wait_rows(place, own, other, scratch, sems, step, per_block):
    wait(row_copies(place, own, other, scratch, sems, step, per_block)[0])


def start(copies):
    for copy in copies:
        copy.start()


def wait(copies):
    for copy in copies:
        copy.wait()


def low_kernel(experts, per_block, place, *refs):
    own, other, refs = refs[:experts], refs[experts : 2 * experts], refs[2 * experts :]
    adapter_in, out, x_scratch, x_sems = refs
    step, steps = pl.program_id(0), pl.num_programs(0)
    pl.when(step == 0)(lambda: start_rows(place, own, other, x_scratch, x_sems, step, per_block))
    pl.when(step + 1 < steps)(lambda: start_rows(place, own, other, x_scratch, x_sems, step + 1, per_block))
    wait_rows(place, own, other, x_scratch, x_sems, step, per_block)
    out[...] = dot(x_scratch[lax.rem(step, 2)], adapter_in[...], 1, 1).astype(bf16)


def low(place, own, other, adapter_in, rows):
    experts = len(own)
    block_rows, share = own[0].shape
    rank = adapter_in.shape[0]
    return pl.pallas_call(
        functools.partial(low_kernel, experts, block_rows // rows),
        out_shape=jax.ShapeDtypeStruct((experts * block_rows, rank), bf16),
        grid_spec=pltpu.PrefetchScalarGridSpec(
            num_scalar_prefetch=1,
            grid=(experts * block_rows // rows,),
            in_specs=[pl.BlockSpec(memory_space=pl.ANY)] * (2 * experts)
            + [pl.BlockSpec(adapter_in.shape, lambda i, place: (0, 0))],
            out_specs=pl.BlockSpec((rows, rank), lambda i, place: (i, 0)),
            scratch_shapes=[pltpu.VMEM((2, rows, 2 * share), bf16), pltpu.SemaphoreType.DMA((2, 2))],
        ),
        compiler_params=pltpu.CompilerParams(vmem_limit_bytes=vmem_limit),
        name="low_rank",
    )(place, *own, *other, adapter_in)


def forward_kernel(experts, per_block, capacity, place, *refs):
    own, other, refs = refs[:experts], refs[experts : 2 * experts], refs[2 * experts :]
    low_rank, adapter_part, parts, refs = refs[0], refs[1], refs[2], refs[3:]
    groups = parts.shape[0]
    hidden, activated, slot_logits, tag_down = refs[:4]
    weight, tag_parts, x_scratch, added, weight_sems, tag_sems, x_sems = refs[4:]
    step, steps = pl.program_id(0), pl.num_programs(0)
    chunks, depth, pair = weight.shape[0], weight.shape[1] // groups, weight.shape[2]
    width, half = pair // 2, tag_parts.shape[2]
    copy = pltpu.make_async_copy

    def weight_copies(chunk):
        for k in range(groups):
            source = parts.at[k, chunk, pl.ds(0, depth)]
            yield copy(source, weight.at[chunk, pl.ds(k * depth, depth)], weight_sems.at[k, chunk])

    def tag_copies():
        for k in range(groups):
            yield copy(parts.at[k, :, pl.ds(depth, half)], tag_parts.at[k], tag_sems.at[k])

    @pl.when(step == 0)
    def _():
        start_rows(place, own, other, x_scratch, x_sems, step, per_block)
        for chunk in range(chunks):
            start(weight_copies(chunk))
        start(tag_copies())

    @pl.when(step + 1 < steps)
    def _():
        start_rows(place, own, other, x_scratch, x_sems, step + 1, per_block)

    @pl.when(step == 0)
    def _():
        for chunk in range(chunks):
            wait(weight_copies(chunk))
        wait(tag_copies())
        summed = jnp.sum(tag_parts[...].astype(f32), axis=0).astype(bf16)
        for chunk in range(chunks):
            columns = slice(chunk * width, (chunk + 1) * width)
            tag_down[:half, columns] = summed[chunk, :, :width]
            tag_down[half:, columns] = summed[chunk, :, width:]

    added[...] = adapter_scale * dot(low_rank[...], adapter_part[...], 1, 0)
    wait_rows(place, own, other, x_scratch, x_sems, step, per_block)
    slot = lax.rem(step, 2)
    for chunk in range(chunks):
        columns = slice(chunk * width, (chunk + 1) * width)
        both = dot(x_scratch[slot], weight[chunk], 1, 0)
        gate_acc = both[:, :width]
        act = gate_acc / (1.0 + jnp.exp(-gate_acc))
        activated[:, columns] = act.astype(bf16)
        hidden[:, columns] = (act * (both[:, width:] + added[:, columns])).astype(bf16)
    slot_logits[...] = jnp.zeros_like(slot_logits)
    logits = dot(tag_down[...], hidden[...], 1, 1).astype(bf16)
    for piece in range(logits.shape[1] // capacity):
        slot_logits[:, piece * lanes : piece * lanes + capacity] = logits[
            :, piece * capacity : (piece + 1) * capacity
        ]


def forward(place, own, other, parts, low_rank, adapter_part, tags, rows, capacity):
    groups, chunks, part_rows, pair = parts.shape
    width, depth = chunks * pair // 2, part_rows - tags // 2
    experts = len(own)
    block_rows, share = own[0].shape
    slots = experts * block_rows
    rank = low_rank.shape[1]
    wide = rows // capacity * lanes
    whole = lambda array: pl.BlockSpec(array.shape, lambda i, place: (0, 0))
    anywhere = pl.BlockSpec(memory_space=pl.ANY)
    return pl.pallas_call(
        functools.partial(forward_kernel, experts, block_rows // rows, capacity),
        out_shape=(
            jax.ShapeDtypeStruct((slots, width), bf16),
            jax.ShapeDtypeStruct((slots, width), bf16),
            jax.ShapeDtypeStruct((tags, slots // capacity * lanes), bf16),
            jax.ShapeDtypeStruct((tags, width), bf16),
        ),
        grid_spec=pltpu.PrefetchScalarGridSpec(
            num_scalar_prefetch=1,
            grid=(slots // rows,),
            in_specs=[anywhere] * (2 * experts)
            + [pl.BlockSpec((rows, rank), lambda i, place: (i, 0)), whole(adapter_part), anywhere],
            out_specs=(
                pl.BlockSpec((rows, width), lambda i, place: (i, 0)),
                pl.BlockSpec((rows, width), lambda i, place: (i, 0)),
                pl.BlockSpec((tags, wide), lambda i, place: (0, i)),
                pl.BlockSpec((tags, width), lambda i, place: (0, 0)),
            ),
            scratch_shapes=[
                pltpu.VMEM((chunks, groups * depth, pair), bf16),
                pltpu.VMEM((groups, chunks, tags // 2, pair), bf16),
                pltpu.VMEM((2, rows, 2 * share), bf16),
                pltpu.VMEM((rows, width), f32),
                pltpu.SemaphoreType.DMA((groups, chunks)),
                pltpu.SemaphoreType.DMA((groups,)),
                pltpu.SemaphoreType.DMA((2, 2)),
            ],
        ),
        compiler_params=pltpu.CompilerParams(vmem_limit_bytes=vmem_limit),
        name="gate_up",
    )(place, *own, *other, low_rank, adapter_part, parts)


def tag_kernel(pieces, *refs):
    parts, (token_logits, combine, labels, slot_grad) = refs[:pieces], refs[pieces:]
    slot_logits = total([part[...] for part in parts])
    logits = token_logits[...] + dot(slot_logits, combine[...], 1, 0, precision=highest)
    exp_logits = jnp.exp(logits)
    probability = exp_logits / jnp.sum(exp_logits, axis=0, keepdims=True)
    hot = labels[...] == lax.broadcasted_iota(jnp.int32, logits.shape, 0)
    logit_grad = probability - jnp.where(hot, f32(1.0), f32(0.0))
    slot_grad[...] = dot(logit_grad, combine[...], 1, 1, precision=highest).astype(bf16)


def column_chunks(count):
    size = min(count, 4 * lanes)
    return [slice(at, at + size) for at in range(0, count, size)]


def down_kernel(first, near_count, capacity, place, hidden, *refs):
    weight, sems = refs[-2:]
    count = sems.shape[0]
    downs, nears, outs = refs[:count], refs[count : count + near_count], refs[count + near_count : -2]
    step, steps = pl.program_id(0), pl.num_programs(0)
    width = downs[0].shape[1]

    @pl.when(step == 0)
    def _():
        copies = []
        for k, down in enumerate(downs):
            column = pl.multiple_of(lax.rem(place[0] ^ (first + k), count) * width, width)
            copies.append(pltpu.make_async_copy(down, weight.at[:, pl.ds(column, width)], sems.at[k]))
        start(copies)
        wait(copies)

    per_step = hidden.shape[0] // capacity
    per_block = 2 * count // per_step

    def multiply(ref):
        for columns in column_chunks(ref.shape[3]):
            value = dot(hidden[...], weight[:, columns], 1, 0).astype(bf16)
            for piece in range(per_step):
                k = lax.rem(step, per_block) * per_step + piece
                ref[place[0] ^ k, 0, :, columns] = value[piece * capacity : (piece + 1) * capacity]

    def far(near, send, keep):
        multiply(send)
        keep[...] = near[...]

    def both(near, send, keep):
        pl.when(place[2] == 0)(lambda: far(near, send, keep))
        pl.when(place[2] == 1)(lambda: far(near, keep, send))

    chunks = near_count or len(outs)
    for chunk in range(chunks):
        if near_count:
            work = functools.partial(both, nears[chunk], outs[chunk], outs[chunks + chunk])
        else:
            work = functools.partial(multiply, outs[chunk])
        pl.when(step // (steps // chunks) == chunk)(work)


def chunk_block(first, count, per_block, step, place):
    return 0, jnp.clip(step - first, 0, count - 1) // per_block, 0, 0


def down(place, hidden, rows, downs, first, nears, chunks, capacity, name):
    slots, (width, part) = hidden.shape[0], downs[0].shape
    share = part * len(downs)
    half = slots // chunks // rows
    results = 2 * chunks if nears else chunks
    groups = 2 * len(downs)
    per_block = groups * capacity // rows
    specs = [
        pl.BlockSpec((groups, 1, capacity, share), functools.partial(chunk_block, chunk * half, half, per_block))
        for chunk in range(chunks)
    ]
    return pl.pallas_call(
        functools.partial(down_kernel, first, len(nears), capacity),
        out_shape=[jax.ShapeDtypeStruct((groups, half // per_block, capacity, share), bf16)] * results,
        grid_spec=pltpu.PrefetchScalarGridSpec(
            num_scalar_prefetch=1,
            grid=(slots // rows,),
            in_specs=[
                pl.BlockSpec((rows, width), lambda i, place: ((chunks - 1 - i // half) * half + lax.rem(i, half), 0))
            ]
            + [pl.BlockSpec(memory_space=pl.ANY)] * len(downs)
            + (specs if nears else []),
            out_specs=specs * (results // chunks),
            scratch_shapes=[pltpu.VMEM((width, share), bf16), pltpu.SemaphoreType.DMA((len(downs),))],
        ),
        compiler_params=pltpu.CompilerParams(vmem_limit_bytes=62 * 1024 * 1024),
        name=name,
    )(place, hidden, *downs, *nears)


def pack_kernel(place, gate, up, down, tag_part, out):
    depth, width = gate.shape
    product = dot(tag_part[...], down[...], 0, 1).astype(bf16)
    half = product.shape[0] // 2
    for chunk in range(width // lanes):
        columns = slice(chunk * lanes, (chunk + 1) * lanes)
        out[0, chunk, :depth, :lanes] = gate[:, columns]
        out[0, chunk, :depth, lanes:] = up[:, columns]
        out[0, chunk, depth:, :lanes] = product[:half, columns]
        out[0, chunk, depth:, lanes:] = product[half:, columns]


def pack(place, gate, up, down, tag_weight, groups):
    depth, width = gate.shape
    part, tags = width // groups, tag_weight.shape[1]
    if part % lanes:
        tag_part = lax.dynamic_slice_in_dim(tag_weight, place[0] * depth, depth, 0)
        product = dot(tag_part, down, 0, 1).astype(bf16)
        rows = [jnp.concatenate([gate, product[: tags // 2]]), jnp.concatenate([up, product[tags // 2 :]])]
        rows = jnp.stack(rows).reshape(2, depth + tags // 2, groups, part)
        return rows.transpose(2, 1, 0, 3).reshape(groups, 1, depth + tags // 2, 2 * part)
    return pl.pallas_call(
        pack_kernel,
        out_shape=jax.ShapeDtypeStruct((groups, part // lanes, depth + tags // 2, 2 * lanes), bf16),
        grid_spec=pltpu.PrefetchScalarGridSpec(
            num_scalar_prefetch=1,
            grid=(groups,),
            in_specs=[
                pl.BlockSpec((depth, part), lambda i, place: (0, i)),
                pl.BlockSpec((depth, part), lambda i, place: (0, i)),
                pl.BlockSpec((part, depth), lambda i, place: (i, 0)),
                pl.BlockSpec((depth, tags), lambda i, place: (place[0], 0)),
            ],
            out_specs=pl.BlockSpec((1, part // lanes, depth + tags // 2, 2 * lanes), lambda i, place: (i, 0, 0, 0)),
        ),
        compiler_params=pltpu.CompilerParams(vmem_limit_bytes=vmem_limit),
        name="pack",
    )(place, gate, up, down, tag_weight)


def backward_kernel(experts, per_block, capacity, place, *refs):
    own, other, refs = refs[:experts], refs[experts : 2 * experts], refs[2 * experts :]
    *slot_grad, tag_down, activated, low_rank, adapter_part, out_grad, in_grad, grads, x_scratch, x_sems = refs
    step, steps = pl.program_id(0), pl.num_programs(0)

    @pl.when(step == 0)
    def _():
        start_rows(place, own, other, x_scratch, x_sems, step, per_block)
        out_grad[...] = jnp.zeros_like(out_grad)
        in_grad[...] = jnp.zeros_like(in_grad)

    @pl.when(step + 1 < steps)
    def _():
        start_rows(place, own, other, x_scratch, x_sems, step + 1, per_block)

    pieces = activated.shape[0] // capacity
    for part in range(per_block):

        @pl.when(lax.rem(step, per_block) == part)
        def _():
            for piece in range(pieces):
                grads[piece] = slot_grad[part * pieces + piece][...]

    hidden_grad = jnp.concatenate([dot(grads[piece][:, :capacity], tag_down[...], 0, 0) for piece in range(pieces)])
    up_grad = (hidden_grad * activated[...].astype(f32)).astype(bf16)
    out_grad[...] += adapter_scale * dot(low_rank[...], up_grad, 0, 0)
    low_grad = (adapter_scale * dot(adapter_part[...], up_grad, 1, 1)).astype(bf16)
    wait_rows(place, own, other, x_scratch, x_sems, step, per_block)
    in_grad[...] += dot(low_grad, x_scratch[lax.rem(step, 2)], 1, 0)


def backward(place, own, other, slot_grad, tag_down, activated, low_rank, adapter_part, rows, capacity):
    experts = len(own)
    block_rows, share = own[0].shape
    per_block = block_rows // rows
    tags, width = tag_down.shape
    slots, rank = low_rank.shape
    whole = lambda shape: pl.BlockSpec(shape, lambda i, place: (0, 0))
    anywhere = pl.BlockSpec(memory_space=pl.ANY)
    return pl.pallas_call(
        functools.partial(backward_kernel, experts, per_block, capacity),
        out_shape=(
            jax.ShapeDtypeStruct((rank, width), f32),
            jax.ShapeDtypeStruct((rank, 2 * share), f32),
        ),
        grid_spec=pltpu.PrefetchScalarGridSpec(
            num_scalar_prefetch=1,
            grid=(slots // rows,),
            in_specs=[anywhere] * (2 * experts)
            + [
                *[pl.BlockSpec((tags, lanes), lambda i, place: (0, i // per_block))] * len(slot_grad),
                whole(tag_down.shape),
                pl.BlockSpec((rows, width), lambda i, place: (i, 0)),
                pl.BlockSpec((rows, rank), lambda i, place: (i, 0)),
                whole(adapter_part.shape),
            ],
            out_specs=(whole((rank, width)), whole((rank, 2 * share))),
            scratch_shapes=[
                pltpu.VMEM((rows // capacity, tags, lanes), bf16),
                pltpu.VMEM((2, rows, 2 * share), bf16),
                pltpu.SemaphoreType.DMA((2, 2)),
            ],
        ),
        compiler_params=pltpu.CompilerParams(vmem_limit_bytes=vmem_limit),
        name="adapter_grad",
    )(place, *own, *other, *slot_grad, tag_down, activated, low_rank, adapter_part)


def finish_kernel(place, *refs):
    both, (in_total, out_total) = refs[:-2], refs[-2:]
    width = in_total.shape[1]
    in_total[...] = total([ref[:, :width] for ref in both])
    part = both[0].shape[1] - width
    for k, ref in enumerate(both):
        column = pl.multiple_of((place[0] ^ k) * part, part)
        out_total[:, pl.ds(column, part)] = ref[:, width:].astype(f32)


def finish(place, both, width):
    rank, part, groups = both[0].shape[0], both[0].shape[1] - width, len(both)
    if part % lanes:
        out_total = jnp.zeros((rank, groups * part), f32)
        for k, value in enumerate(both):
            value = value[:, width:].astype(f32)
            out_total = lax.dynamic_update_slice_in_dim(out_total, value, (place[0] ^ k) * part, 1)
        return total([value[:, :width] for value in both]), out_total
    whole = lambda shape: pl.BlockSpec(shape, lambda i, place: (0, 0))
    shapes = (rank, width), (rank, groups * part)
    return pl.pallas_call(
        finish_kernel,
        out_shape=[jax.ShapeDtypeStruct(shape, f32) for shape in shapes],
        grid_spec=pltpu.PrefetchScalarGridSpec(
            num_scalar_prefetch=1,
            grid=(1,),
            in_specs=[whole(value.shape) for value in both],
            out_specs=[whole(shape) for shape in shapes],
        ),
        compiler_params=pltpu.CompilerParams(vmem_limit_bytes=vmem_limit),
        name="finish",
    )(place, *both)


def local(
    tokens,
    expert_ids,
    gate_values,
    tag_labels,
    w_gate,
    w_up,
    w_down,
    adapter_in,
    adapter_out,
    tag_weight,
):
    experts = lax.axis_size("expert")
    groups = lax.axis_size("dp")
    dp, expert, tensor = lax.axis_index("dp"), lax.axis_index("expert"), lax.axis_index("tensor")
    upper = dp // (groups // 2)
    place = jnp.stack([dp, tensor, upper ^ tensor]).astype(jnp.int32)
    tok_count, model_width = tokens.shape
    share_width = model_width // lax.axis_size("tensor")
    capacity = 3 * tok_count // experts
    feature_part = w_gate.shape[1]
    hidden_part = w_gate.shape[2] // groups
    tags = tag_weight.shape[1]
    rank = adapter_in.shape[1]
    block_rows = groups * capacity
    rows = 4 * capacity

    member = expert_ids[None, :, :] == jnp.arange(experts, dtype=jnp.int32)[:, None, None]
    used = jnp.any(member, axis=2).astype(f32)
    weight = jnp.sum(jnp.where(member, gate_values[None], f32(0.0)), axis=2)
    upto = (jnp.arange(tok_count)[:, None] <= jnp.arange(tok_count)[None, :]).astype(f32)
    code = used * dot(used, upto, 1, 0)
    steps = sorted(range(experts), key=lambda step: (step % 2, step))
    order = jnp.array(steps, jnp.int32) ^ expert
    places = jnp.arange(1, lanes + 1, dtype=jnp.int32).astype(f32)
    own_match = code[order][:, None, :] == places[None, :, None]
    combine = jnp.where(own_match, weight[order][:, None, :], f32(0.0)).reshape(experts * lanes, tok_count)

    token_half = lax.dynamic_slice_in_dim(tokens, tensor * share_width, share_width, 1)
    code_rows = jnp.pad(code.astype(bf16), ((0, 8 - experts), (0, share_width - tok_count)))
    plane = gather(jnp.concatenate([token_half, code_rows], axis=0), "dp")
    parts = pack(place, w_gate[0], w_up[0], w_down[0], tag_weight, groups)
    plane_parts = plane
    plane = jnp.stack(plane)
    plane_code = plane[:, tok_count : tok_count + experts, :tok_count].astype(f32)
    plane_tokens = plane[:, :tok_count]
    downs = [lax.dynamic_slice_in_dim(w_down[0], (dp ^ k) * hidden_part, hidden_part, 0) for k in range(groups)]
    plane_tokens = after(plane_tokens, parts, *downs)
    parts = lax.all_to_all(after(parts, *plane_parts), "dp", split_axis=0, concat_axis=0, tiled=True)
    x_own = []
    for j in steps:
        target_code = lax.dynamic_index_in_dim(plane_code, expert ^ j, 1, keepdims=False)
        match = (target_code[:, None, :] == places[None, :capacity, None]).astype(bf16)
        outgoing = jnp.einsum("gst,gtd->gsd", match, plane_tokens, preferred_element_type=f32).astype(bf16)
        x_own.append(outgoing.reshape(block_rows, share_width))
    x_own = swap(x_own, "expert", steps)
    x_other = [send(value, "tensor", 1) for value in x_own]
    low_rank = low(place, x_own, x_other, adapter_in[0], rows)
    token_logits = dot(tag_weight, tokens, 0, 1)
    parts = after(parts, low_rank, combine, token_logits)
    downs = swap([after(piece, parts) for piece in downs], "dp")
    adapter_part = lax.dynamic_slice_in_dim(adapter_out[0], dp * hidden_part, hidden_part, 1)

    hidden, activated, slot_logits, tag_down = forward(
        place, x_own, x_other, parts, low_rank, adapter_part, tags, rows, capacity
    )

    slot_logits = (slot_logits.astype(f32) + send(slot_logits, "tensor", 1).astype(f32)).astype(bf16)
    plane_lanes = groups * lanes
    pieces = [slot_logits[:, j * plane_lanes : (j + 1) * plane_lanes] for j in range(experts)]
    pieces = swap(pieces, "expert", steps)

    chunks = [(experts // 2, experts // 2), (0, experts // 2)]
    half = groups // 2

    def change(part):
        return lax.all_to_all(part, "dp", split_axis=0, concat_axis=0, tiled=True)

    near = down(place, hidden, rows, downs[:half], 0, [], len(chunks), capacity, "down_near")
    hidden = after(hidden, near[0], *pieces)
    pieces = [
        jnp.concatenate([piece[:, k * lanes : (k + 1) * lanes] for piece in pieces], axis=1) for k in range(groups)
    ]
    pieces = swap(pieces, "dp")
    halves = down(place, hidden, rows, downs[half:], half, near, len(chunks), capacity, "down_far")
    others, kept = [send(value, "tensor", 1) for value in halves[: len(chunks)]], halves[len(chunks) :]

    def own(chunk, came):
        value = (kept[chunk].astype(f32) + came.astype(f32)).astype(bf16)
        return value.reshape(groups, -1, share_width)

    first = own(0, others[0])

    pieces[0] = after(pieces[0], first)
    slot_grad = pl.pallas_call(
        functools.partial(tag_kernel, groups),
        out_shape=jax.ShapeDtypeStruct((tags, experts * lanes), bf16),
        compiler_params=pltpu.CompilerParams(vmem_limit_bytes=vmem_limit),
        name="tag_grad",
    )(*pieces, token_logits, combine, tag_labels[None, :])
    slot_grad = swap([slot_grad[:, j * lanes : (j + 1) * lanes] for j in range(experts)], "expert", steps)
    second = own(1, after(others[1], *slot_grad))
    slot_grad = gather(jnp.concatenate(slot_grad, axis=1), "dp")
    came = [change(after(first, *pieces)), change(after(second, *slot_grad[1:]))]

    sums = [jnp.sum(came[0].astype(f32), axis=0).astype(bf16)]
    slot_grad[0] = after(slot_grad[0], sums[0])
    out_local, in_local = backward(
        place, x_own, x_other, slot_grad, tag_down, activated, low_rank, adapter_part, rows, capacity
    )
    returned = [None] * experts

    def give_back(chunk):
        first, count = chunks[chunk]
        for j in range(first, first + count):
            kept = sums[chunk][(j - first) * capacity : (j - first + 1) * capacity]
            returned[j] = send(kept, "expert", steps[j]) if steps[j] else kept

    give_back(0)
    in_local = after(in_local, *returned[chunks[0][0] :])
    in_local = in_local + send(in_local.astype(bf16), "tensor", 1).astype(f32)
    both = gather(jnp.concatenate([in_local, out_local], axis=1).astype(bf16), "dp")
    for j in range(chunks[1][1] - 1, -1, -1):
        value = came[1][:, j * capacity : (j + 1) * capacity]
        value = jnp.sum(value.astype(f32), axis=0).astype(bf16)
        returned[j] = send(value, "expert", steps[j]) if steps[j] else after(value, both[0])
        both[0] = after(both[0], value) if steps[j] else both[0]
    in_total, out_total = finish(place, both, model_width)
    layer_out = token_half.astype(f32)
    for j in range(experts):
        kept = combine[j * lanes : j * lanes + capacity]
        layer_out = layer_out + dot(kept, returned[j].astype(f32), 0, 0, precision=highest)
    layer_out = layer_out.astype(bf16)
    return (layer_out, in_total[None], out_total[None])


def solution(mesh):
    in_specs = (
        P(("dp", "expert"), None),
        P(("dp", "expert"), None),
        P(("dp", "expert"), None),
        P(("dp", "expert")),
        P("expert", "dp", "tensor"),
        P("expert", "dp", "tensor"),
        P("expert", "tensor", "dp"),
        P("expert", None, None),
        P("expert", None, "tensor"),
        P(),
    )
    out_specs = (
        P(("dp", "expert"), "tensor"),
        P("expert", None, None),
        P("expert", None, "tensor"),
    )
    return jax.shard_map(local, mesh=mesh, in_specs=in_specs, out_specs=out_specs, check_vma=False)
```
